32 devices in a mesh: req: 8 (over z, x), head: 4 (over y, core).
Axes of the slice: x: 2, y: 2, z: 4, core: 2. Of those that a mesh axis runs over, the one named last changes fastest.
Arguments:
- prompt_query_latents: bfloat16 [4096, 1536], P(('req', 'head')), may hold values from -6 to 6
- prompt_latents: bfloat16 [4096, 512], P(('req', 'head')), may hold values from -320 to 320
- prompt_rotary_keys: bfloat16 [64, 4096], P(None, ('req', 'head')), may hold values from -6 to 6
- positions: int32 [4096], P(('req', 'head')), may hold values from 0 to 511, as said below
- query_up_weight: bfloat16 [1536, 12288], P(None, 'head'), may hold values from -0.15625 to 0.15625
- key_up_weight: bfloat16 [512, 8192], P(None, 'head'), may hold values from -0.25 to 0.25
- value_up_weight: bfloat16 [512, 8192], P(None, 'head'), may hold values from -0.25 to 0.25
- decode_queries: bfloat16 [512, 12288], P('req', 'head'), may hold values from -6 to 6
- decode_owner_index: int32 [512], P('req'), may hold values from 0 to 7, as said below
- decode_cache_slot: int32 [512], P('req'), may hold values from 0 to 63, as said below
- latent_cache_rows: bfloat16 [512, 256, 512], P('req'), may hold values from -320 to 320
- rotated_cache_keys: bfloat16 [512, 64, 256], P('req'), may hold values from -6 to 6
- cache_live_lengths: int32 [512], P('req'), may hold values from 1 to 256
Outputs:
- prompt_attention_output: bfloat16 [4096, 8192], P('req', 'head')
- decode_out: bfloat16 [512, 8192], P('req', 'head')
The draws below stay inside these ranges and needn't reach their ends.
Inputs may be any that keep to these rules, and one draw needn't show every extreme that they name: `positions`: a position is 0 where a prompt begins, always at the first token of a block and, from the second block on, at other tokens too, and otherwise one more than the previous token's; the first block holds one whole prompt. `decode_owner_index`: each entry device's 64 requests name 4 owners, each exactly 16 times; every pair of owner and slot is named by exactly one request. `decode_cache_slot`: see decode_owner_index.
All inputs are finite; a program needn't handle non-finite values.
Results may differ from the reference program's by a relative error of at most 0.012.
The reference program's roundings to bfloat16 on the way count: a program that leaves them out, or rounds other values in their place, can miss the bound.
Values may be sent and summed in bfloat16 or wider, within the bound.
A program may use at most 192 MiB of HBM per device.

```python
import jax
import jax.numpy as jnp
from jax import lax

H = 64
QUERY_LATENT = 1536
D_C = 512
D_NOPE = 128
D_ROPE = 64
D_V = 128
PROMPT_BLOCK = 512
PROMPT_TOKENS = 4096
DEC_DEV = 64
DEC_ROWS = 512
MOST = 16
CMAX = 256
N_REQ = 8


def routing_tables(key):
    group_count = DEC_DEV // MOST
    key_one, key_two, key_three = jax.random.split(key, 3)
    owner_order = jax.random.permutation(key_one, N_REQ)
    offsets = jax.random.permutation(key_two, N_REQ)[:group_count]
    source = jnp.arange(N_REQ, dtype=jnp.int32)[:, None]
    column = jnp.arange(DEC_DEV, dtype=jnp.int32)[None, :]
    group_index = column // MOST
    owner_table = owner_order[(source + offsets[group_index]) % N_REQ]
    slot_table = jnp.broadcast_to(column, (N_REQ, DEC_DEV))
    shuffle = jax.random.permutation(key_three, slot_table, axis=1, independent=True)
    owner_table = jnp.take_along_axis(owner_table, shuffle, axis=1).reshape(-1)
    slot_table = jnp.take_along_axis(slot_table, shuffle, axis=1).reshape(-1)
    return (owner_table.astype(jnp.int32), slot_table.astype(jnp.int32))


def draw_decode_owner_index(key, part):
    return routing_tables(key)[0]


def draw_decode_cache_slot(key, part):
    return routing_tables(key)[1]


def draw_cache_live_lengths(key, part):
    key = jax.random.fold_in(key, 5)
    key_one, key_two, key_three = jax.random.split(key, 3)
    factor = jax.random.randint(key_one, (N_REQ, 1), 1, 5)
    raw_draw = jax.random.randint(key_two, (N_REQ, DEC_DEV), 0, CMAX)
    lengths = (1 + raw_draw * factor // 4).reshape(-1)
    chosen = jax.random.randint(key_three, (), 0, DEC_ROWS)
    lengths = jnp.where(jnp.arange(DEC_ROWS) == chosen, CMAX, lengths)
    return lengths.astype(jnp.int32)


def draw_positions(key, part):
    key = jax.random.fold_in(key, 7)
    token_index = jnp.arange(PROMPT_TOKENS, dtype=jnp.int32)
    starts = jax.random.randint(key, (PROMPT_TOKENS,), 0, max(PROMPT_BLOCK // 2, 2))
    begins = (starts == 0) & (token_index >= PROMPT_BLOCK) | (token_index % PROMPT_BLOCK == 0)
    last_begin = lax.cummax(jnp.where(begins, token_index, 0), axis=0)
    return (token_index - last_begin).astype(jnp.int32)


def latent_draw(key, shape):
    key_one = jax.random.fold_in(key, 0)
    base_draw = jax.random.normal(key_one, shape, jnp.float32)
    return jnp.clip(base_draw, -320.0, 320.0).astype(jnp.bfloat16)


def draw_latent_cache_rows(key, part):
    key = jax.random.fold_in(key, 11)
    return latent_draw(key, (DEC_ROWS, CMAX, D_C))


def draw_prompt_latents(key, part):
    key = jax.random.fold_in(key, 13)
    return latent_draw(key, (PROMPT_TOKENS, D_C))


def block_levels(stream_key, extent, cuts, low, top_value):
    level = 1.0
    for dim, shards_of in cuts:
        heights = jax.random.uniform(jax.random.fold_in(jax.random.fold_in(stream_key, 6), dim), (shards_of,), jnp.float32, low / len(cuts), top_value / len(cuts))
        level = level * jnp.repeat(jnp.exp(heights), extent[dim] // shards_of).reshape((-1,) + (1,) * (len(extent) - 1 - dim))
    return level


def scatter_about(rng, dims, scale, bound, shards=(), kind=jnp.bfloat16):
    gain = block_levels(rng, dims, shards, -0.22, 0.18) if shards else 1.0
    values = jax.random.normal(rng, dims, jnp.float32) * scale * gain
    return jnp.minimum(jnp.maximum(values, -bound), bound).astype(kind)


def setup_inputs(seed: int = 0) -> dict:
    keys = jax.random.split(jax.random.key(seed), 14)
    return {
        "prompt_query_latents": scatter_about(keys[0], (PROMPT_TOKENS, QUERY_LATENT), 1.0, 6.0, ((0, 32),)),
        "prompt_latents": draw_prompt_latents(jax.random.fold_in(keys[13], 71), 0),
        "prompt_rotary_keys": scatter_about(keys[2], (D_ROPE, PROMPT_TOKENS), 1.0, 6.0, ((1, 32),)),
        "positions": draw_positions(jax.random.fold_in(keys[13], 71), 0),
        "query_up_weight": scatter_about(keys[4], (QUERY_LATENT, H * (D_NOPE + D_ROPE)), QUERY_LATENT ** -0.5, 0.15625, ((1, 4),)),
        "key_up_weight": scatter_about(keys[5], (D_C, H * D_NOPE), D_C ** -0.5, 0.25, ((1, 4),)),
        "value_up_weight": scatter_about(keys[6], (D_C, H * D_V), D_C ** -0.5, 0.25, ((1, 4),)),
        "decode_queries": scatter_about(keys[7], (DEC_ROWS, H * (D_NOPE + D_ROPE)), 1.0, 6.0, ((0, 8), (1, 4))),
        "decode_owner_index": draw_decode_owner_index(jax.random.fold_in(keys[13], 71), 0),
        "decode_cache_slot": draw_decode_cache_slot(jax.random.fold_in(keys[13], 71), 0),
        "latent_cache_rows": draw_latent_cache_rows(jax.random.fold_in(keys[13], 71), 0),
        "rotated_cache_keys": scatter_about(keys[11], (DEC_ROWS, D_ROPE, CMAX), 1.0, 6.0, ((0, 8),)),
        "cache_live_lengths": draw_cache_live_lengths(jax.random.fold_in(keys[13], 71), 0),
    }


ROPE_BASE = 10000.0


def rotate(values, position):
    half_width = values.shape[-1] // 2
    frequency = ROPE_BASE ** (-jnp.arange(half_width, dtype=jnp.float32) / half_width)
    angles = position.astype(jnp.float32)[..., None] * frequency
    cosines = jnp.cos(angles)
    sine_term = jnp.sin(angles)
    first_half = values[..., :half_width]
    second_half = values[..., half_width:]
    return jnp.concatenate([first_half * cosines - second_half * sine_term, first_half * sine_term + second_half * cosines], axis=-1)


def rounded(values):
    return lax.optimization_barrier(values.astype(jnp.bfloat16)).astype(jnp.float32)


def reference(prompt_query_latents, prompt_latents, prompt_rotary_keys, positions, query_up_weight, key_up_weight, value_up_weight, decode_queries, decode_owner_index, decode_cache_slot, latent_cache_rows, rotated_cache_keys, cache_live_lengths):
    score_scale = (D_NOPE + D_ROPE) ** -0.5

    def prefill_block(pieces):
        query_rows, latent_rows, rope_cols, block_place = pieces
        queries = jnp.dot(query_rows, query_up_weight, preferred_element_type=jnp.float32).reshape(PROMPT_BLOCK, H, D_NOPE + D_ROPE)
        query_rope = rotate(queries[..., D_NOPE:], block_place[:, None])
        queries = rounded(jnp.concatenate([queries[..., :D_NOPE], query_rope], axis=-1))
        key_nope = rounded(jnp.dot(latent_rows, key_up_weight, preferred_element_type=jnp.float32)).reshape(PROMPT_BLOCK, H, D_NOPE)
        value_rows = rounded(jnp.dot(latent_rows, value_up_weight, preferred_element_type=jnp.float32)).reshape(PROMPT_BLOCK, H, D_V)
        key_rope = rounded(rotate(rope_cols.T.astype(jnp.float32), block_place))
        scores = (jnp.einsum('shd,thd->hst', queries[..., :D_NOPE], key_nope) + jnp.einsum('shd,td->hst', queries[..., D_NOPE:], key_rope)) * score_scale
        token_index = jnp.arange(PROMPT_BLOCK, dtype=jnp.int32)
        visible = (token_index[None, :] <= token_index[:, None]) & (token_index[None, :] >= token_index[:, None] - block_place[:, None])
        scores = jnp.where(visible[None], scores, -jnp.inf)
        weights = rounded(jax.nn.softmax(scores, axis=-1))
        return jnp.einsum('hst,thd->shd', weights, value_rows).astype(jnp.bfloat16).reshape(PROMPT_BLOCK, H * D_V)

    prompt_attention_output = lax.map(prefill_block, (
        prompt_query_latents.reshape(N_REQ, PROMPT_BLOCK, QUERY_LATENT),
        prompt_latents.reshape(N_REQ, PROMPT_BLOCK, D_C),
        prompt_rotary_keys.reshape(D_ROPE, N_REQ, PROMPT_BLOCK).transpose(1, 0, 2),
        positions.reshape(N_REQ, PROMPT_BLOCK))).reshape(PROMPT_TOKENS, H * D_V)

    key_map = key_up_weight.astype(jnp.float32).reshape(D_C, H, D_NOPE)
    value_map = value_up_weight.astype(jnp.float32).reshape(D_C, H, D_V)
    cache_index = (decode_owner_index * DEC_DEV + decode_cache_slot).astype(jnp.int32)

    def decode_row(pieces):
        query_row, cache_row = pieces
        query_heads = query_row.astype(jnp.float32).reshape(H, D_NOPE + D_ROPE)
        latent_query = rounded(jnp.einsum('hd,chd->hc', query_heads[:, :D_NOPE], key_map))
        latent = lax.dynamic_index_in_dim(latent_cache_rows, cache_row, 0, keepdims=False).astype(jnp.float32)
        rope_rows = lax.dynamic_index_in_dim(rotated_cache_keys, cache_row, 0, keepdims=False).astype(jnp.float32)
        length = lax.dynamic_index_in_dim(cache_live_lengths, cache_row, 0, keepdims=False)
        scores = (jnp.einsum('hc,tc->ht', latent_query, latent) + jnp.einsum('hd,dt->ht', query_heads[:, D_NOPE:], rope_rows)) * score_scale
        visible = jnp.arange(CMAX, dtype=jnp.int32) < length
        scores = jnp.where(visible[None, :], scores, -jnp.inf)
        weights = rounded(jax.nn.softmax(scores, axis=-1))
        latent_out = rounded(jnp.einsum('ht,tc->hc', weights, latent))
        return jnp.einsum('hc,chd->hd', latent_out, value_map).astype(jnp.bfloat16).reshape(H * D_V)

    decode_out = lax.map(decode_row, (decode_queries, cache_index))
    return prompt_attention_output, decode_out
```

```python
import functools
import math

import jax
import jax.numpy as jnp
from jax import lax
from jax.experimental import pallas as pl
from jax.experimental.pallas import tpu as pltpu
from jax.sharding import PartitionSpec as P

D_C = 512
D_NOPE = 128
D_ROPE = 64
D_V = 128
D_Q = D_NOPE + D_ROPE
ROPE_BASE = 10000.0
SCALE = D_Q ** (-0.5)
EXP2_SCALE = SCALE * math.log2(math.e)
MASKED = -1e30
DIGIT = 256
NT = (((1,), (1,)), ((), ()))
TN = (((0,), (0,)), ((), ()))
VMEM_BYTES = 56 * 1024 * 1024


def mm(a, b, dims=(((1,), (0,)), ((), ()))):
    return lax.dot_general(a, b, dims, preferred_element_type=jnp.float32)


def softmax_weights(scores):
    shifted = scores - jnp.max(scores, axis=-1, keepdims=True)
    grown = jnp.exp2(shifted * EXP2_SCALE)
    total = jnp.sum(grown, axis=-1, keepdims=True)
    return (grown * (1.0 / total)).astype(jnp.bfloat16)


def decode_kernel(
    slots_per_step,
    head_count,
    lengths_ref,
    payload_ref,
    key_up_ref,
    value_up_ref,
    cache_ref,
    rope_ref,
    out_ref,
    nope_ref,
    rope_query_ref,
):
    step = pl.program_id(0)
    width = head_count * D_Q
    slot_count = nope_ref.shape[0]
    rows = slots_per_step * head_count

    @pl.when(step == 0)
    def _():
        requests = payload_ref.shape[0]
        owner = payload_ref[:, width : width + 1].astype(jnp.float32)
        slot = payload_ref[:, width + 1 : width + 2].astype(jnp.float32)
        me = lax.axis_index("req").astype(jnp.float32)
        lanes = lax.broadcasted_iota(jnp.int32, (requests, slot_count), 1).astype(jnp.float32)
        chosen = jnp.where((owner == me) & (slot == lanes), 1.0, 0.0).astype(jnp.bfloat16)
        for head in range(head_count):
            columns = mm(chosen, payload_ref[:, head * D_Q : (head + 1) * D_Q], TN)
            nope_ref[:, head * D_NOPE : (head + 1) * D_NOPE] = columns[:, :D_NOPE]
            rope_query_ref[:, head * D_ROPE : (head + 1) * D_ROPE] = columns[:, D_NOPE:]

    first = pl.multiple_of(step * slots_per_step, slots_per_step)

    def spread(values, unit):
        shape = (slots_per_step, head_count, head_count * unit)
        own = lax.broadcasted_iota(jnp.int32, shape, 1) == (
            lax.broadcasted_iota(jnp.int32, shape, 2) // unit
        )
        wide = jnp.where(own, jnp.broadcast_to(values[:, None, :], shape), 0.0)
        return wide.reshape(rows, head_count * unit).astype(jnp.bfloat16), own

    nope, own_head = spread(nope_ref[pl.ds(first, slots_per_step), :], D_NOPE)
    latent_query = mm(nope, key_up_ref[...], NT).astype(jnp.bfloat16)
    ropes, _ = spread(rope_query_ref[pl.ds(first, slots_per_step), :], D_ROPE)
    fold = (
        lax.broadcasted_iota(jnp.int32, (head_count * D_ROPE, D_ROPE), 0) % D_ROPE
        == lax.broadcasted_iota(jnp.int32, (head_count * D_ROPE, D_ROPE), 1)
    )
    rope_query = mm(ropes, jnp.where(fold, 1.0, 0.0).astype(jnp.bfloat16)).astype(jnp.bfloat16)

    lanes = lax.broadcasted_iota(jnp.int32, (head_count, cache_ref.shape[1]), 1)
    parts = []
    for item in range(slots_per_step):
        latent = cache_ref[item]
        place = slice(item * head_count, (item + 1) * head_count)
        scores = mm(latent_query[place], latent, NT) + mm(rope_query[place], rope_ref[item])
        scores = jnp.where(lanes < lengths_ref[first + item], scores, MASKED)
        parts.append(mm(softmax_weights(scores), latent).astype(jnp.bfloat16))
    latent_out = jnp.concatenate(parts, axis=0)
    raised = mm(latent_out, value_up_ref[...]).reshape(
        slots_per_step, head_count, head_count * D_V
    )
    out_ref[...] = jnp.sum(jnp.where(own_head, raised, 0.0), axis=1).astype(jnp.bfloat16)


def decode_attention(payload, key_up, value_up, cache, rope_cache, lengths):
    slot_count, cache_rows, _ = cache.shape
    head_count = key_up.shape[1] // D_NOPE
    per_step = 8
    whole = lambda step, *_: (0, 0)
    flops = 2 * slot_count * head_count * (
        2 * head_count * D_NOPE * D_C + 2 * cache_rows * D_C + cache_rows * D_ROPE
    )
    return pl.pallas_call(
        functools.partial(decode_kernel, per_step, head_count),
        out_shape=jax.ShapeDtypeStruct((slot_count, head_count * D_V), jnp.bfloat16),
        grid_spec=pltpu.PrefetchScalarGridSpec(
            num_scalar_prefetch=1,
            grid=(slot_count // per_step,),
            in_specs=[
                pl.BlockSpec(payload.shape, whole),
                pl.BlockSpec(key_up.shape, whole),
                pl.BlockSpec(value_up.shape, whole),
                pl.BlockSpec((per_step, cache_rows, D_C), lambda step, *_: (step, 0, 0)),
                pl.BlockSpec((per_step, D_ROPE, cache_rows), lambda step, *_: (step, 0, 0)),
            ],
            out_specs=pl.BlockSpec((per_step, head_count * D_V), lambda step, *_: (step, 0)),
            scratch_shapes=[
                pltpu.VMEM((slot_count, head_count * D_NOPE), jnp.float32),
                pltpu.VMEM((slot_count, head_count * D_ROPE), jnp.float32),
            ],
        ),
        compiler_params=pltpu.CompilerParams(vmem_limit_bytes=VMEM_BYTES),
        cost_estimate=pl.CostEstimate(
            flops=flops, bytes_accessed=cache.size * 2 + payload.size * 2, transcendentals=0
        ),
    )(lengths, payload, key_up, value_up, cache, rope_cache)


def prefill_kernel(
    query_latents_ref,
    latents_ref,
    extras_ref,
    cosines_ref,
    sines_ref,
    query_up_ref,
    key_up_ref,
    value_up_ref,
    out_ref,
    bias_ref,
    key_rope_ref,
):
    tokens = query_latents_ref.shape[0]
    lanes = lax.broadcasted_iota(jnp.int32, (tokens, D_NOPE), 1)
    low = lanes < D_ROPE

    def rotated(values):
        swapped = jnp.where(
            lanes % D_ROPE < D_ROPE // 2,
            pltpu.roll(values, D_NOPE - D_ROPE // 2, 1),
            pltpu.roll(values, D_ROPE // 2, 1),
        )
        return values * cosines_ref[...] + swapped * sines_ref[...]

    @pl.when(pl.program_id(0) == 0)
    def _():
        extras = extras_ref[...].astype(jnp.float32)
        position = extras[:, D_ROPE : D_ROPE + 1] * DIGIT + extras[:, D_ROPE + 1 : D_ROPE + 2]
        row = lax.broadcasted_iota(jnp.int32, (tokens, tokens), 0).astype(jnp.float32)
        column = lax.broadcasted_iota(jnp.int32, (tokens, tokens), 1).astype(jnp.float32)
        visible = (column <= row) & (column >= row - position)
        bias_ref[...] = jnp.where(visible, 0.0, MASKED)
        twice = jnp.where(low, extras, pltpu.roll(extras, D_ROPE, 1))
        key_rope_ref[...] = rotated(twice).astype(jnp.bfloat16)

    projected = mm(query_latents_ref[...], query_up_ref[...])
    left = projected[:, :D_NOPE].astype(jnp.bfloat16)
    middle = projected[:, D_NOPE : 2 * D_NOPE]
    middle = jnp.where(low, rotated(middle), middle).astype(jnp.bfloat16)
    right = projected[:, 2 * D_NOPE :]
    right = jnp.where(low, right, rotated(right)).astype(jnp.bfloat16)
    keys = mm(latents_ref[...], key_up_ref[...])
    values = mm(latents_ref[...], value_up_ref[...]).astype(jnp.bfloat16)
    key_rope = key_rope_ref[...].astype(jnp.float32)
    turned = pltpu.roll(keys[:, D_NOPE:], D_ROPE, 1)
    pairs = (
        (
            jnp.concatenate([left, middle], axis=1),
            jnp.concatenate([keys[:, :D_NOPE], jnp.where(low, key_rope, 0.0)], axis=1),
        ),
        (
            jnp.concatenate([middle, right], axis=1),
            jnp.concatenate(
                [jnp.where(low, 0.0, turned), jnp.where(low, turned, key_rope)], axis=1
            ),
        ),
    )
    tile = 128
    for head, (query, key) in enumerate(pairs):
        key = key.astype(jnp.bfloat16)
        value = values[:, head * D_V : (head + 1) * D_V]
        for begin in range(0, tokens, tile):
            end = begin + tile
            scores = mm(query[begin:end], key[:end], NT) + bias_ref[begin:end, :end]
            weights = softmax_weights(scores)
            out_ref[begin:end, head * D_V : (head + 1) * D_V] = mm(weights, value[:end]).astype(
                jnp.bfloat16
            )


def prefill_attention(gathered, cosines, sines, query_up, key_up, value_up):
    tokens = gathered.shape[0]
    latent_width = query_up.shape[0]
    head_count = key_up.shape[1] // D_NOPE
    extra_block = (latent_width + D_C) // D_NOPE
    whole = lambda step: (0, 0)
    across = lambda step: (0, step)
    flops = 2 * tokens * head_count * (latent_width * D_Q + 2 * D_C * D_NOPE + tokens * 384)
    return pl.pallas_call(
        prefill_kernel,
        out_shape=jax.ShapeDtypeStruct((tokens, head_count * D_V), jnp.bfloat16),
        grid=(head_count // 2,),
        in_specs=[
            pl.BlockSpec((tokens, latent_width), whole),
            pl.BlockSpec((tokens, D_C), lambda step: (0, latent_width // D_C)),
            pl.BlockSpec((tokens, D_NOPE), lambda step: (0, extra_block)),
            pl.BlockSpec((tokens, D_NOPE), whole),
            pl.BlockSpec((tokens, D_NOPE), whole),
            pl.BlockSpec((latent_width, 2 * D_Q), across),
            pl.BlockSpec((D_C, 2 * D_NOPE), across),
            pl.BlockSpec((D_C, 2 * D_V), across),
        ],
        out_specs=pl.BlockSpec((tokens, 2 * D_V), across),
        scratch_shapes=[
            pltpu.VMEM((tokens, tokens), jnp.float32),
            pltpu.VMEM((tokens, D_NOPE), jnp.bfloat16),
        ],
        compiler_params=pltpu.CompilerParams(vmem_limit_bytes=VMEM_BYTES),
        cost_estimate=pl.CostEstimate(
            flops=flops, bytes_accessed=query_up.size * 2 + key_up.size * 4, transcendentals=0
        ),
    )(gathered, gathered, gathered, cosines, sines, query_up, key_up, value_up)


def rope_tables(position):
    half_width = D_ROPE // 2
    frequency = ROPE_BASE ** (-jnp.arange(half_width, dtype=jnp.float32) / half_width)
    angles = position.astype(jnp.float32)[:, None] * frequency
    cosines, sines = jnp.cos(angles), jnp.sin(angles)
    return (
        jnp.concatenate([cosines] * 4, axis=1),
        jnp.concatenate([-sines, sines] * 2, axis=1),
    )


def on_device(
    prompt_query_latents,
    prompt_latents,
    prompt_rotary_keys,
    positions,
    query_up_weight,
    key_up_weight,
    value_up_weight,
    decode_queries,
    decode_owner_index,
    decode_cache_slot,
    latent_cache_rows,
    rotated_cache_keys,
    cache_live_lengths,
):
    row_count = decode_queries.shape[0]
    slot_count = latent_cache_rows.shape[0]
    token_count = prompt_latents.shape[0]

    def digits(first, second, rows, width):
        lane = lax.broadcasted_iota(jnp.int32, (rows, width), 1)
        return jnp.where(
            lane == 0, first[:, None], jnp.where(lane == 1, second[:, None], 0)
        ).astype(jnp.bfloat16)

    payload = jnp.concatenate(
        [decode_queries, digits(decode_owner_index, decode_cache_slot, row_count, 128)], axis=1
    )
    payload = lax.all_gather(payload, "req", axis=0, tiled=True)
    prompt = jnp.concatenate(
        [
            prompt_query_latents,
            prompt_latents,
            prompt_rotary_keys.T,
            digits(positions // DIGIT, positions % DIGIT, token_count, 64),
        ],
        axis=1,
    )
    prompt = lax.all_gather(prompt, "head", axis=0, tiled=True)

    answers = decode_attention(
        payload,
        key_up_weight,
        value_up_weight,
        latent_cache_rows,
        rotated_cache_keys,
        cache_live_lengths,
    )
    returned = lax.all_gather(answers, "req", axis=0, tiled=True)
    prompt, answers = lax.optimization_barrier((prompt, answers))

    place = prompt_query_latents.shape[1] + D_C + D_ROPE
    high_low = prompt[:, place : place + 2].astype(jnp.int32)
    cosines, sines = rope_tables(high_low[:, 0] * DIGIT + high_low[:, 1])
    prompt_attention_output = prefill_attention(
        prompt, cosines, sines, query_up_weight, key_up_weight, value_up_weight
    )
    cache_index = decode_owner_index * slot_count + decode_cache_slot
    wanted = (
        cache_index[:, None] == jnp.arange(returned.shape[0], dtype=jnp.int32)[None, :]
    ).astype(jnp.bfloat16)
    decode_out = jnp.dot(wanted, returned, preferred_element_type=jnp.float32).astype(
        jnp.bfloat16
    )
    return (prompt_attention_output, decode_out)


def solution(mesh):
    placed = (
        P(("req", "head"), None),
        P(("req", "head"), None),
        P(None, ("req", "head")),
        P(("req", "head")),
        P(None, "head"),
        P(None, "head"),
        P(None, "head"),
        P("req", "head"),
        P("req"),
        P("req"),
        P("req", None, None),
        P("req", None, None),
        P("req"),
    )
    return jax.shard_map(
        on_device,
        mesh=mesh,
        in_specs=placed,
        out_specs=(P("req", "head"), P("req", "head")),
        check_vma=False,
    )
```

```python
import functools
import math

import jax
import jax.numpy as jnp
from jax import lax
from jax.experimental import pallas as pl
from jax.experimental.pallas import tpu as pltpu
from jax.sharding import PartitionSpec as P

D_C = 512
D_NOPE = 128
D_ROPE = 64
D_V = 128
D_Q = D_NOPE + D_ROPE
ROPE_BASE = 10000.0
SCALE = D_Q ** (-0.5)
EXP2_SCALE = SCALE * math.log2(math.e)
MASKED = -1e30
DIGIT = 256
NT = (((1,), (1,)), ((), ()))
TN = (((0,), (0,)), ((), ()))
VMEM_BYTES = 56 * 1024 * 1024


def mm(a, b, dims=(((1,), (0,)), ((), ()))):
    return lax.dot_general(a, b, dims, preferred_element_type=jnp.float32)


def softmax_weights(scores):
    shifted = scores - jnp.max(scores, axis=-1, keepdims=True)
    grown = jnp.exp2(shifted * EXP2_SCALE)
    total = jnp.sum(grown, axis=-1, keepdims=True)
    return (grown * (1.0 / total)).astype(jnp.bfloat16)


def send_kernel(peers, most, owner_ref, slot_ref, queries_ref, payload_ref, back_ref):
    rows, width = queries_ref.shape
    owner = owner_ref[...].astype(jnp.float32)
    slot = slot_ref[...].astype(jnp.float32)
    across = jnp.broadcast_to(owner, (rows, rows))
    down = across.T
    before = lax.broadcasted_iota(jnp.int32, (rows, rows), 0) < lax.broadcasted_iota(
        jnp.int32, (rows, rows), 1
    )
    rank = jnp.sum(jnp.where((across == down) & before, 1.0, 0.0), axis=0, keepdims=True)
    me = lax.axis_index("req").astype(jnp.float32)
    hops = me - owner
    hops = jnp.where(hops < 0, hops + peers, hops)
    back_ref[...] = (hops * most + rank).astype(jnp.int32)
    index = lax.broadcasted_iota(jnp.int32, (peers * most, rows), 0).astype(jnp.float32)
    placing = index == owner * most + rank
    payload_ref[:, :width] = mm(
        jnp.where(placing, 1.0, 0.0).astype(jnp.bfloat16), queries_ref[...]
    ).astype(jnp.bfloat16)
    code = jnp.sum(jnp.where(placing, slot + 1.0, 0.0), axis=1, keepdims=True)
    payload_ref[:, width:] = jnp.broadcast_to(code, (peers * most, 128)).astype(jnp.bfloat16)


def pack_queries(queries, owner, slot, peers, most):
    rows, width = queries.shape
    return pl.pallas_call(
        functools.partial(send_kernel, peers, most),
        out_shape=(
            jax.ShapeDtypeStruct((peers * most, width + 128), jnp.bfloat16),
            jax.ShapeDtypeStruct((1, rows), jnp.int32),
        ),
        compiler_params=pltpu.CompilerParams(vmem_limit_bytes=VMEM_BYTES),
    )(owner[None, :], slot[None, :], queries)


def collect_kernel(back_ref, *refs):
    block_refs, out_ref = refs[:-1], refs[-1]
    blocks = jnp.concatenate([ref[...].astype(jnp.float32) for ref in block_refs], axis=0)
    index = lax.broadcasted_iota(jnp.int32, (blocks.shape[0], back_ref.shape[1]), 0)
    wanted = jnp.where(index == back_ref[...], 1.0, 0.0).astype(jnp.bfloat16)
    out_ref[...] = mm(wanted, blocks.astype(jnp.bfloat16), TN).astype(jnp.bfloat16)


def collect(back, blocks):
    return pl.pallas_call(
        collect_kernel,
        out_shape=jax.ShapeDtypeStruct((back.shape[1], blocks[0].shape[1]), jnp.bfloat16),
        compiler_params=pltpu.CompilerParams(vmem_limit_bytes=VMEM_BYTES),
    )(back, *blocks)


def decode_kernel(
    slots_per_step,
    head_count,
    peers,
    lengths_ref,
    payload_ref,
    key_up_ref,
    value_up_ref,
    cache_ref,
    rope_ref,
    *refs,
):
    out_refs, (query_ref, rope_query_ref, latent_out_ref) = refs[:peers], refs[peers:]
    step = pl.program_id(0)
    width = head_count * D_Q
    slot_count = query_ref.shape[1] // head_count
    chunks = query_ref.shape[0]
    rows = slots_per_step * head_count
    items = payload_ref.shape[0]

    def chosen():
        code = payload_ref[:, width : width + 1].astype(jnp.float32)
        slots = lax.broadcasted_iota(jnp.int32, (items, slot_count), 1).astype(jnp.float32)
        return jnp.where(code == slots + 1.0, 1.0, 0.0).astype(jnp.bfloat16)

    @pl.when(step == 0)
    def _():
        queries = mm(chosen(), payload_ref[:, :width], TN)
        for head in range(head_count):
            nope = queries[:, head * D_Q : head * D_Q + D_NOPE].astype(jnp.bfloat16)
            latent = mm(nope, key_up_ref[:, head * D_NOPE : (head + 1) * D_NOPE], NT)
            place = pl.ds(head, slot_count, stride=head_count)
            latent = latent.astype(jnp.bfloat16).astype(jnp.float32)
            for chunk in range(chunks):
                query_ref[chunk, place, :] = latent[:, chunk * 128 : (chunk + 1) * 128]
            rope = queries[:, head * D_Q + D_NOPE : (head + 1) * D_Q]
            rope_query_ref[place, :] = jnp.concatenate([rope, rope], axis=1)

    first = pl.multiple_of(step * slots_per_step, slots_per_step)
    here = pl.ds(pl.multiple_of(step * rows, rows), rows)
    columns = jnp.concatenate(
        [query_ref[chunk, here, :].T for chunk in range(chunks)], axis=0
    ).astype(jnp.bfloat16)
    rope_query = rope_query_ref[here, :D_ROPE].astype(jnp.bfloat16)
    owner = lax.broadcasted_iota(jnp.int32, columns.shape, 1) // head_count
    none = jnp.zeros_like(columns)
    turned = None
    for item in range(slots_per_step):
        part = mm(cache_ref[item], jnp.where(owner == item, columns, none))
        turned = part if turned is None else turned + part
    scores = turned.T
    lanes = lax.broadcasted_iota(jnp.int32, (head_count, cache_ref.shape[1]), 1)
    parts = []
    for item in range(slots_per_step):
        place = slice(item * head_count, (item + 1) * head_count)
        part = scores[place] + mm(rope_query[place], rope_ref[item])
        parts.append(jnp.where(lanes < lengths_ref[first + item], part, MASKED))
    weights = softmax_weights(jnp.concatenate(parts, axis=0))
    for item in range(slots_per_step):
        place = slice(item * head_count, (item + 1) * head_count)
        latent = mm(weights[place], cache_ref[item]).astype(jnp.bfloat16).astype(jnp.float32)
        below = pl.ds(pl.multiple_of(step * rows, rows) + item * head_count, head_count)
        for chunk in range(chunks):
            latent_out_ref[chunk, below, :] = latent[:, chunk * 128 : (chunk + 1) * 128]

    @pl.when(step == pl.num_programs(0) - 1)
    def _():
        me = lax.axis_index("req")
        most = items // peers
        source = lax.broadcasted_iota(jnp.int32, (items, items), 0) + me * most
        source = jnp.where(source >= items, source - items, source)
        order = source == lax.broadcasted_iota(jnp.int32, (items, items), 1)
        sending = mm(jnp.where(order, 1.0, 0.0).astype(jnp.bfloat16), chosen())
        sending = sending.astype(jnp.bfloat16)
        for head in range(head_count):
            strided = pl.ds(head, slot_count, stride=head_count)
            latent = jnp.concatenate(
                [latent_out_ref[chunk, strided, :] for chunk in range(chunks)], axis=1
            )
            place = slice(head * D_V, (head + 1) * D_V)
            answer = mm(latent.astype(jnp.bfloat16), value_up_ref[:, place])
            answer = mm(sending, answer.astype(jnp.bfloat16)).astype(jnp.bfloat16)
            for peer in range(peers):
                out_refs[peer][:, place] = answer[peer * most : (peer + 1) * most]


def decode_attention(payload, key_up, value_up, cache, rope_cache, lengths, peers):
    slot_count, cache_rows, _ = cache.shape
    head_count = key_up.shape[1] // D_NOPE
    per_step = 8
    most = payload.shape[0] // peers
    whole = lambda step, *_: (0, 0)
    flops = 2 * slot_count * head_count * (2 * D_NOPE * D_C + 17 * cache_rows * D_C)
    block = jax.ShapeDtypeStruct((most, head_count * D_V), jnp.bfloat16)
    return pl.pallas_call(
        functools.partial(decode_kernel, per_step, head_count, peers),
        out_shape=(block,) * peers,
        grid_spec=pltpu.PrefetchScalarGridSpec(
            num_scalar_prefetch=1,
            grid=(slot_count // per_step,),
            in_specs=[
                pl.BlockSpec(payload.shape, whole),
                pl.BlockSpec(key_up.shape, whole),
                pl.BlockSpec(value_up.shape, whole),
                pl.BlockSpec((per_step, cache_rows, D_C), lambda step, *_: (step, 0, 0)),
                pl.BlockSpec((per_step, D_ROPE, cache_rows), lambda step, *_: (step, 0, 0)),
            ],
            out_specs=(pl.BlockSpec(block.shape, whole),) * peers,
            scratch_shapes=[
                pltpu.VMEM((D_C // 128, slot_count * head_count, 128), jnp.float32),
                pltpu.VMEM((slot_count * head_count, 2 * D_ROPE), jnp.float32),
                pltpu.VMEM((D_C // 128, slot_count * head_count, 128), jnp.float32),
            ],
        ),
        compiler_params=pltpu.CompilerParams(vmem_limit_bytes=VMEM_BYTES),
        cost_estimate=pl.CostEstimate(
            flops=flops, bytes_accessed=cache.size * 2 + payload.size * 2, transcendentals=0
        ),
    )(lengths, payload, key_up, value_up, cache, rope_cache)


def prefill_kernel(
    heads,
    query_latents_ref,
    latents_ref,
    extras_ref,
    frequency_ref,
    query_up_ref,
    key_up_ref,
    value_up_ref,
    out_ref,
    bias_ref,
    cosine_ref,
    sine_ref,
    key_rope_ref,
):
    tokens = query_latents_ref.shape[0]
    lanes = lax.broadcasted_iota(jnp.int32, (tokens, D_NOPE), 1)
    low = lanes < D_ROPE
    leading = lanes % D_ROPE < D_ROPE // 2

    def rotated(values):
        swapped = jnp.where(
            leading,
            pltpu.roll(values, D_NOPE - D_ROPE // 2, 1),
            pltpu.roll(values, D_ROPE // 2, 1),
        )
        return values * cosine_ref[...] + swapped * sine_ref[...]

    @pl.when(pl.program_id(0) == 0)
    def _():
        extras = extras_ref[...].astype(jnp.float32)
        position = extras[:, D_ROPE : D_ROPE + 1] * DIGIT + extras[:, D_ROPE + 1 : D_ROPE + 2]
        row = lax.broadcasted_iota(jnp.int32, (tokens, tokens), 0).astype(jnp.float32)
        column = lax.broadcasted_iota(jnp.int32, (tokens, tokens), 1).astype(jnp.float32)
        visible = (column <= row) & (column >= row - position)
        bias_ref[...] = jnp.where(visible, 0.0, MASKED)
        angles = position * frequency_ref[...]
        cosine_ref[...] = jnp.cos(angles)
        sines = jnp.sin(angles)
        sine_ref[...] = jnp.where(leading, -sines, sines)
        twice = jnp.where(low, extras, pltpu.roll(extras, D_ROPE, 1))
        key_rope_ref[...] = rotated(twice).T[:D_ROPE].astype(jnp.bfloat16)

    projected = mm(query_latents_ref[...], query_up_ref[...])
    keys = mm(latents_ref[...], key_up_ref[...]).astype(jnp.bfloat16).T
    values = mm(latents_ref[...], value_up_ref[...]).astype(jnp.bfloat16)
    key_rope = key_rope_ref[...]
    none = jnp.zeros((D_ROPE, tokens), jnp.bfloat16)
    tile = 128
    for pair in range(heads // 2):
        base = pair * 2 * D_Q
        left = projected[:, base : base + D_NOPE].astype(jnp.bfloat16)
        middle = projected[:, base + D_NOPE : base + 2 * D_NOPE]
        middle = jnp.where(low, rotated(middle), middle).astype(jnp.bfloat16)
        right = projected[:, base + 2 * D_NOPE : base + 3 * D_NOPE]
        right = jnp.where(low, right, rotated(right)).astype(jnp.bfloat16)
        even = keys[2 * pair * D_NOPE : (2 * pair + 1) * D_NOPE]
        odd = keys[(2 * pair + 1) * D_NOPE : (2 * pair + 2) * D_NOPE]
        both = (
            (
                jnp.concatenate([left, middle], axis=1),
                jnp.concatenate([even, key_rope, none], axis=0),
            ),
            (
                jnp.concatenate([middle, right], axis=1),
                jnp.concatenate([none, odd, key_rope], axis=0),
            ),
        )
        for side, (query, key) in enumerate(both):
            place = slice((2 * pair + side) * D_V, (2 * pair + side + 1) * D_V)
            value = values[:, place]
            for begin in range(0, tokens, tile):
                end = begin + tile
                scores = mm(query[begin:end], key[:, :end]) + bias_ref[begin:end, :end]
                weights = softmax_weights(scores)
                out_ref[begin:end, place] = mm(weights, value[:end]).astype(jnp.bfloat16)


def prefill_attention(gathered, query_up, key_up, value_up):
    tokens = gathered.shape[0]
    latent_width = query_up.shape[0]
    head_count = key_up.shape[1] // D_NOPE
    extra_block = (latent_width + D_C) // D_NOPE
    heads = 4
    half_width = D_ROPE // 2
    frequency = ROPE_BASE ** (-jnp.arange(half_width, dtype=jnp.float32) / half_width)
    whole = lambda step: (0, 0)
    across = lambda step: (0, step)
    flops = 2 * tokens * head_count * (latent_width * D_Q + 2 * D_C * D_NOPE + tokens * 384)
    return pl.pallas_call(
        functools.partial(prefill_kernel, heads),
        out_shape=jax.ShapeDtypeStruct((tokens, head_count * D_V), jnp.bfloat16),
        grid=(head_count // heads,),
        in_specs=[
            pl.BlockSpec((tokens, latent_width), whole),
            pl.BlockSpec((tokens, D_C), lambda step: (0, latent_width // D_C)),
            pl.BlockSpec((tokens, D_NOPE), lambda step: (0, extra_block)),
            pl.BlockSpec((1, D_NOPE), whole),
            pl.BlockSpec((latent_width, heads * D_Q), across),
            pl.BlockSpec((D_C, heads * D_NOPE), across),
            pl.BlockSpec((D_C, heads * D_V), across),
        ],
        out_specs=pl.BlockSpec((tokens, heads * D_V), across),
        scratch_shapes=[
            pltpu.VMEM((tokens, tokens), jnp.float32),
            pltpu.VMEM((tokens, D_NOPE), jnp.float32),
            pltpu.VMEM((tokens, D_NOPE), jnp.float32),
            pltpu.VMEM((D_ROPE, tokens), jnp.bfloat16),
        ],
        compiler_params=pltpu.CompilerParams(vmem_limit_bytes=VMEM_BYTES),
        cost_estimate=pl.CostEstimate(
            flops=flops, bytes_accessed=query_up.size * 2 + key_up.size * 4, transcendentals=0
        ),
    )(
        gathered,
        gathered,
        gathered,
        jnp.tile(frequency, 4)[None, :],
        query_up,
        key_up,
        value_up,
    )


def on_device(
    prompt_query_latents,
    prompt_latents,
    prompt_rotary_keys,
    positions,
    query_up_weight,
    key_up_weight,
    value_up_weight,
    decode_queries,
    decode_owner_index,
    decode_cache_slot,
    latent_cache_rows,
    rotated_cache_keys,
    cache_live_lengths,
):
    row_count = decode_queries.shape[0]
    token_count = prompt_latents.shape[0]
    peers = lax.axis_size("req")
    most = max(2, row_count * 2 // peers)

    lane = lax.broadcasted_iota(jnp.int32, (token_count, D_ROPE), 1)
    place = positions[:, None]
    digits = jnp.where(lane == 0, place // DIGIT, jnp.where(lane == 1, place % DIGIT, 0))
    prompt = jnp.concatenate(
        [
            prompt_query_latents,
            prompt_latents,
            prompt_rotary_keys.T,
            digits.astype(jnp.bfloat16),
        ],
        axis=1,
    )
    prompt = lax.all_gather(prompt, "head", axis=0, tiled=True)

    payload, back = pack_queries(
        decode_queries, decode_owner_index, decode_cache_slot, peers, most
    )
    payload = lax.all_to_all(
        payload.reshape(peers, most, -1), "req", split_axis=0, concat_axis=0, tiled=True
    ).reshape(peers * most, -1)
    answers = decode_attention(
        payload,
        key_up_weight,
        value_up_weight,
        latent_cache_rows,
        rotated_cache_keys,
        cache_live_lengths,
        peers,
    )
    returned = [answers[0]] + [
        lax.ppermute(answers[hop], "req", [(i, (i + hop) % peers) for i in range(peers)])
        for hop in range(1, peers)
    ]
    prompt, _ = lax.optimization_barrier((prompt, answers[0]))
    prompt_attention_output = prefill_attention(
        prompt, query_up_weight, key_up_weight, value_up_weight
    )
    back, prompt_attention_output = lax.optimization_barrier((back, prompt_attention_output))
    return (prompt_attention_output, collect(back, returned))


def solution(mesh):
    placed = (
        P(("req", "head"), None),
        P(("req", "head"), None),
        P(None, ("req", "head")),
        P(("req", "head")),
        P(None, "head"),
        P(None, "head"),
        P(None, "head"),
        P("req", "head"),
        P("req"),
        P("req"),
        P("req", None, None),
        P("req", None, None),
        P("req"),
    )
    return jax.shard_map(
        on_device,
        mesh=mesh,
        in_specs=placed,
        out_specs=(P("req", "head"), P("req", "head")),
        check_vma=False,
    )
```

```python
import functools
import math

import jax
import jax.numpy as jnp
from jax import lax
from jax.experimental import pallas as pl
from jax.experimental.pallas import tpu as pltpu
from jax.sharding import PartitionSpec as P

D_C = 512
D_NOPE = 128
D_ROPE = 64
D_V = 128
D_Q = D_NOPE + D_ROPE
ROPE_BASE = 10000.0
SCALE = D_Q ** (-0.5)
EXP2_SCALE = SCALE * math.log2(math.e)
MASKED = -1e30
DIGIT = 256
NT = (((1,), (1,)), ((), ()))
TN = (((0,), (0,)), ((), ()))
VMEM_BYTES = 56 * 1024 * 1024


def mm(a, b, dims=(((1,), (0,)), ((), ()))):
    return lax.dot_general(a, b, dims, preferred_element_type=jnp.float32)


def softmax_weights(scores):
    shifted = scores - jnp.max(scores, axis=-1, keepdims=True)
    grown = jnp.exp2(shifted * EXP2_SCALE)
    total = jnp.sum(grown, axis=-1, keepdims=True)
    return (grown * (1.0 / total)).astype(jnp.bfloat16)


def exchange(peers, source_ref, target_ref, local_sem, send_sem, recv_sem):
    me = lax.axis_index("req")
    barrier = pltpu.get_barrier_semaphore()
    for hop in range(1, peers):
        pl.semaphore_signal(
            barrier,
            inc=1,
            device_id={"req": lax.rem(me + hop, peers)},
            device_id_type=pl.DeviceIdType.MESH,
        )
    pl.semaphore_wait(barrier, peers - 1)
    copies = []
    for hop in range(1, peers):
        target = lax.rem(me + hop, peers)
        copy = pltpu.make_async_remote_copy(
            src_ref=source_ref.at[target],
            dst_ref=target_ref.at[me],
            send_sem=send_sem.at[hop],
            recv_sem=recv_sem.at[hop],
            device_id={"req": target},
            device_id_type=pl.DeviceIdType.MESH,
        )
        copy.start()
        copies.append(copy)
    own = pltpu.make_async_copy(source_ref.at[me], target_ref.at[me], local_sem)
    own.start()
    own.wait()
    for copy in copies:
        copy.wait()


def send_kernel(
    owner_ref, slot_ref, queries_ref, payload_ref, back_ref, packed_ref, local_sem, send_sem, recv_sem
):
    peers, most, _ = payload_ref.shape
    rows, width = queries_ref.shape
    owner = owner_ref[...].astype(jnp.float32)
    slot = slot_ref[...].astype(jnp.float32)
    across = jnp.broadcast_to(owner, (rows, rows))
    down = across.T
    before = lax.broadcasted_iota(jnp.int32, (rows, rows), 0) < lax.broadcasted_iota(
        jnp.int32, (rows, rows), 1
    )
    rank = jnp.sum(jnp.where((across == down) & before, 1.0, 0.0), axis=0, keepdims=True)
    place = owner * most + rank
    back_ref[...] = place.astype(jnp.int32)
    index = lax.broadcasted_iota(jnp.int32, (peers * most, rows), 0).astype(jnp.float32)
    placing = index == place
    packed = mm(jnp.where(placing, 1.0, 0.0).astype(jnp.bfloat16), queries_ref[...])
    code = jnp.sum(jnp.where(placing, slot + 1.0, 0.0), axis=1, keepdims=True)
    packed_ref[:, :, :width] = packed.reshape(peers, most, width).astype(jnp.bfloat16)
    packed_ref[:, :, width:] = (
        jnp.broadcast_to(code, (peers * most, 128)).reshape(peers, most, 128).astype(jnp.bfloat16)
    )
    exchange(peers, packed_ref, payload_ref, local_sem, send_sem, recv_sem)


def exchange_sems(peers):
    return [
        pltpu.SemaphoreType.DMA,
        pltpu.SemaphoreType.DMA((peers,)),
        pltpu.SemaphoreType.DMA((peers,)),
    ]


def send_queries(queries, owner, slot, peers, most):
    rows, width = queries.shape
    vmem = pl.BlockSpec(memory_space=pltpu.VMEM)
    return pl.pallas_call(
        send_kernel,
        out_shape=(
            jax.ShapeDtypeStruct((peers, most, width + 128), jnp.bfloat16),
            jax.ShapeDtypeStruct((1, rows), jnp.int32),
        ),
        in_specs=[vmem] * 3,
        out_specs=(pl.BlockSpec(memory_space=pl.ANY), vmem),
        scratch_shapes=[pltpu.VMEM((peers, most, width + 128), jnp.bfloat16)]
        + exchange_sems(peers),
        compiler_params=pltpu.CompilerParams(
            vmem_limit_bytes=VMEM_BYTES, collective_id=0, has_side_effects=True
        ),
    )(owner[None, :], slot[None, :], queries)


def collect_kernel(back_ref, answers_ref, out_ref, landed_ref, local_sem, send_sem, recv_sem):
    peers, most, width = landed_ref.shape
    exchange(peers, answers_ref, landed_ref, local_sem, send_sem, recv_sem)
    blocks = landed_ref[...].astype(jnp.float32).reshape(peers * most, width)
    index = lax.broadcasted_iota(jnp.int32, (peers * most, back_ref.shape[1]), 0)
    wanted = jnp.where(index == back_ref[...], 1.0, 0.0).astype(jnp.bfloat16)
    out_ref[...] = mm(wanted, blocks.astype(jnp.bfloat16), TN).astype(jnp.bfloat16)


def return_answers(back, answers):
    peers = answers.shape[0]
    vmem = pl.BlockSpec(memory_space=pltpu.VMEM)
    return pl.pallas_call(
        collect_kernel,
        out_shape=jax.ShapeDtypeStruct((back.shape[1], answers.shape[2]), jnp.bfloat16),
        in_specs=[vmem, pl.BlockSpec(memory_space=pl.ANY)],
        out_specs=vmem,
        scratch_shapes=[pltpu.VMEM(answers.shape, jnp.bfloat16)] + exchange_sems(peers),
        compiler_params=pltpu.CompilerParams(
            vmem_limit_bytes=VMEM_BYTES, collective_id=1, has_side_effects=True
        ),
    )(back, answers)


def decode_kernel(
    slots_per_step,
    head_count,
    lengths_ref,
    payload_ref,
    key_up_ref,
    value_up_ref,
    cache_ref,
    rope_ref,
    out_ref,
    query_ref,
    rope_query_ref,
    latent_out_ref,
):
    step = pl.program_id(0)
    width = head_count * D_Q
    slot_count = query_ref.shape[1] // head_count
    chunks = query_ref.shape[0]
    rows = slots_per_step * head_count
    peers, most, _ = payload_ref.shape
    items = peers * most

    def chosen():
        code = payload_ref[:, :, width:].astype(jnp.float32).reshape(items, 128)[:, :1]
        slots = lax.broadcasted_iota(jnp.int32, (items, slot_count), 1).astype(jnp.float32)
        return jnp.where(code == slots + 1.0, 1.0, 0.0).astype(jnp.bfloat16)

    @pl.when(step == 0)
    def _():
        received = payload_ref[:, :, :width].reshape(items, width)
        queries = mm(chosen(), received, TN)
        for head in range(head_count):
            nope = queries[:, head * D_Q : head * D_Q + D_NOPE].astype(jnp.bfloat16)
            latent = mm(nope, key_up_ref[:, head * D_NOPE : (head + 1) * D_NOPE], NT)
            place = pl.ds(head, slot_count, stride=head_count)
            latent = latent.astype(jnp.bfloat16).astype(jnp.float32)
            for chunk in range(chunks):
                query_ref[chunk, place, :] = latent[:, chunk * 128 : (chunk + 1) * 128]
            rope = queries[:, head * D_Q + D_NOPE : (head + 1) * D_Q]
            rope_query_ref[place, :] = jnp.concatenate([rope, rope], axis=1)

    first = pl.multiple_of(step * slots_per_step, slots_per_step)
    here = pl.ds(pl.multiple_of(step * rows, rows), rows)
    columns = jnp.concatenate(
        [query_ref[chunk, here, :].T for chunk in range(chunks)], axis=0
    ).astype(jnp.bfloat16)
    rope_query = rope_query_ref[here, :D_ROPE].astype(jnp.bfloat16)
    owner = lax.broadcasted_iota(jnp.int32, columns.shape, 1) // head_count
    none = jnp.zeros_like(columns)
    turned = None
    for item in range(slots_per_step):
        part = mm(cache_ref[item], jnp.where(owner == item, columns, none))
        turned = part if turned is None else turned + part
    scores = turned.T
    lanes = lax.broadcasted_iota(jnp.int32, (head_count, cache_ref.shape[1]), 1)
    parts = []
    for item in range(slots_per_step):
        place = slice(item * head_count, (item + 1) * head_count)
        part = scores[place] + mm(rope_query[place], rope_ref[item])
        parts.append(jnp.where(lanes < lengths_ref[first + item], part, MASKED))
    weights = softmax_weights(jnp.concatenate(parts, axis=0))
    for item in range(slots_per_step):
        place = slice(item * head_count, (item + 1) * head_count)
        latent = mm(weights[place], cache_ref[item]).astype(jnp.bfloat16).astype(jnp.float32)
        below = pl.ds(pl.multiple_of(step * rows, rows) + item * head_count, head_count)
        for chunk in range(chunks):
            latent_out_ref[chunk, below, :] = latent[:, chunk * 128 : (chunk + 1) * 128]

    @pl.when(step == pl.num_programs(0) - 1)
    def _():
        sending = chosen()
        for head in range(head_count):
            strided = pl.ds(head, slot_count, stride=head_count)
            latent = jnp.concatenate(
                [latent_out_ref[chunk, strided, :] for chunk in range(chunks)], axis=1
            )
            place = slice(head * D_V, (head + 1) * D_V)
            answer = mm(latent.astype(jnp.bfloat16), value_up_ref[:, place])
            answer = mm(sending, answer.astype(jnp.bfloat16)).astype(jnp.bfloat16)
            out_ref[:, :, place] = answer.reshape(peers, most, D_V)


def decode_attention(payload, key_up, value_up, cache, rope_cache, lengths):
    slot_count, cache_rows, _ = cache.shape
    head_count = key_up.shape[1] // D_NOPE
    per_step = 8
    peers, most, _ = payload.shape
    whole = lambda step, *_: (0, 0)
    single = lambda step, *_: (0, 0, 0)
    flops = 2 * slot_count * head_count * (2 * D_NOPE * D_C + 17 * cache_rows * D_C)
    block = jax.ShapeDtypeStruct((peers, most, head_count * D_V), jnp.bfloat16)
    return pl.pallas_call(
        functools.partial(decode_kernel, per_step, head_count),
        out_shape=block,
        grid_spec=pltpu.PrefetchScalarGridSpec(
            num_scalar_prefetch=1,
            grid=(slot_count // per_step,),
            in_specs=[
                pl.BlockSpec(payload.shape, single),
                pl.BlockSpec(key_up.shape, whole),
                pl.BlockSpec(value_up.shape, whole),
                pl.BlockSpec((per_step, cache_rows, D_C), lambda step, *_: (step, 0, 0)),
                pl.BlockSpec((per_step, D_ROPE, cache_rows), lambda step, *_: (step, 0, 0)),
            ],
            out_specs=pl.BlockSpec(block.shape, single),
            scratch_shapes=[
                pltpu.VMEM((D_C // 128, slot_count * head_count, 128), jnp.float32),
                pltpu.VMEM((slot_count * head_count, 2 * D_ROPE), jnp.float32),
                pltpu.VMEM((D_C // 128, slot_count * head_count, 128), jnp.float32),
            ],
        ),
        compiler_params=pltpu.CompilerParams(vmem_limit_bytes=VMEM_BYTES),
        cost_estimate=pl.CostEstimate(
            flops=flops, bytes_accessed=cache.size * 2 + payload.size * 2, transcendentals=0
        ),
    )(lengths, payload, key_up, value_up, cache, rope_cache)


def prefill_kernel(
    heads,
    query_latents_ref,
    latents_ref,
    extras_ref,
    frequency_ref,
    query_up_ref,
    key_up_ref,
    value_up_ref,
    out_ref,
    bias_ref,
    cosine_ref,
    sine_ref,
    key_rope_ref,
):
    tokens = query_latents_ref.shape[0]
    lanes = lax.broadcasted_iota(jnp.int32, (tokens, D_NOPE), 1)
    low = lanes < D_ROPE
    leading = lanes % D_ROPE < D_ROPE // 2

    def rotated(values):
        swapped = jnp.where(
            leading,
            pltpu.roll(values, D_NOPE - D_ROPE // 2, 1),
            pltpu.roll(values, D_ROPE // 2, 1),
        )
        return values * cosine_ref[...] + swapped * sine_ref[...]

    @pl.when(pl.program_id(0) == 0)
    def _():
        extras = extras_ref[...].astype(jnp.float32)
        position = extras[:, D_ROPE : D_ROPE + 1] * DIGIT + extras[:, D_ROPE + 1 : D_ROPE + 2]
        row = lax.broadcasted_iota(jnp.int32, (tokens, tokens), 0).astype(jnp.float32)
        column = lax.broadcasted_iota(jnp.int32, (tokens, tokens), 1).astype(jnp.float32)
        visible = (column <= row) & (column >= row - position)
        bias_ref[...] = jnp.where(visible, 0.0, MASKED)
        angles = position * frequency_ref[...]
        cosine_ref[...] = jnp.cos(angles)
        sines = jnp.sin(angles)
        sine_ref[...] = jnp.where(leading, -sines, sines)
        twice = jnp.where(low, extras, pltpu.roll(extras, D_ROPE, 1))
        key_rope_ref[...] = rotated(twice).T[:D_ROPE].astype(jnp.bfloat16)

    projected = mm(query_latents_ref[...], query_up_ref[...])
    keys = mm(latents_ref[...], key_up_ref[...]).astype(jnp.bfloat16).T
    values = mm(latents_ref[...], value_up_ref[...]).astype(jnp.bfloat16)
    key_rope = key_rope_ref[...]
    none = jnp.zeros((D_ROPE, tokens), jnp.bfloat16)
    tile = min(256, tokens)
    work = []
    for pair in range(heads // 2):
        base = pair * 2 * D_Q
        left = projected[:, base : base + D_NOPE].astype(jnp.bfloat16)
        middle = projected[:, base + D_NOPE : base + 2 * D_NOPE]
        middle = jnp.where(low, rotated(middle), middle).astype(jnp.bfloat16)
        right = projected[:, base + 2 * D_NOPE : base + 3 * D_NOPE]
        right = jnp.where(low, right, rotated(right)).astype(jnp.bfloat16)
        even = keys[2 * pair * D_NOPE : (2 * pair + 1) * D_NOPE]
        odd = keys[(2 * pair + 1) * D_NOPE : (2 * pair + 2) * D_NOPE]
        both = (
            (
                jnp.concatenate([left, middle], axis=1),
                jnp.concatenate([even, key_rope, none], axis=0),
            ),
            (
                jnp.concatenate([middle, right], axis=1),
                jnp.concatenate([none, odd, key_rope], axis=0),
            ),
        )
        for side, (query, key) in enumerate(both):
            place = slice((2 * pair + side) * D_V, (2 * pair + side + 1) * D_V)
            for begin in range(0, tokens, tile):
                work.append((query, key, place, begin, begin + tile))

    def score(query, key, place, begin, end):
        return mm(query[begin:end], key[:, :end]) + bias_ref[begin:end, :end]

    scores = score(*work[0])
    for index, (_, _, place, begin, end) in enumerate(work):
        following = score(*work[index + 1]) if index + 1 < len(work) else None
        weights = softmax_weights(scores)
        out_ref[begin:end, place] = mm(weights, values[:end, place]).astype(jnp.bfloat16)
        scores = following


def prefill_attention(gathered, query_up, key_up, value_up):
    tokens = gathered.shape[0]
    latent_width = query_up.shape[0]
    head_count = key_up.shape[1] // D_NOPE
    extra_block = (latent_width + D_C) // D_NOPE
    heads = 4
    half_width = D_ROPE // 2
    frequency = ROPE_BASE ** (-jnp.arange(half_width, dtype=jnp.float32) / half_width)
    whole = lambda step: (0, 0)
    across = lambda step: (0, step)
    flops = 2 * tokens * head_count * (latent_width * D_Q + 2 * D_C * D_NOPE + tokens * 384)
    return pl.pallas_call(
        functools.partial(prefill_kernel, heads),
        out_shape=jax.ShapeDtypeStruct((tokens, head_count * D_V), jnp.bfloat16),
        grid=(head_count // heads,),
        in_specs=[
            pl.BlockSpec((tokens, latent_width), whole),
            pl.BlockSpec((tokens, D_C), lambda step: (0, latent_width // D_C)),
            pl.BlockSpec((tokens, D_NOPE), lambda step: (0, extra_block)),
            pl.BlockSpec((1, D_NOPE), whole),
            pl.BlockSpec((latent_width, heads * D_Q), across),
            pl.BlockSpec((D_C, heads * D_NOPE), across),
            pl.BlockSpec((D_C, heads * D_V), across),
        ],
        out_specs=pl.BlockSpec((tokens, heads * D_V), across),
        scratch_shapes=[
            pltpu.VMEM((tokens, tokens), jnp.float32),
            pltpu.VMEM((tokens, D_NOPE), jnp.float32),
            pltpu.VMEM((tokens, D_NOPE), jnp.float32),
            pltpu.VMEM((D_ROPE, tokens), jnp.bfloat16),
        ],
        compiler_params=pltpu.CompilerParams(vmem_limit_bytes=VMEM_BYTES),
        cost_estimate=pl.CostEstimate(
            flops=flops, bytes_accessed=query_up.size * 2 + key_up.size * 4, transcendentals=0
        ),
    )(
        gathered,
        gathered,
        gathered,
        jnp.tile(frequency, 4)[None, :],
        query_up,
        key_up,
        value_up,
    )


def on_device(
    prompt_query_latents,
    prompt_latents,
    prompt_rotary_keys,
    positions,
    query_up_weight,
    key_up_weight,
    value_up_weight,
    decode_queries,
    decode_owner_index,
    decode_cache_slot,
    latent_cache_rows,
    rotated_cache_keys,
    cache_live_lengths,
):
    row_count = decode_queries.shape[0]
    token_count = prompt_latents.shape[0]
    peers = lax.axis_size("req")
    most = max(2, row_count * 2 // peers)

    lane = lax.broadcasted_iota(jnp.int32, (token_count, D_ROPE), 1)
    place = positions[:, None]
    digits = jnp.where(lane == 0, place // DIGIT, jnp.where(lane == 1, place % DIGIT, 0))
    prompt = jnp.concatenate(
        [
            prompt_query_latents,
            prompt_latents,
            prompt_rotary_keys.T,
            digits.astype(jnp.bfloat16),
        ],
        axis=1,
    )
    prompt = lax.all_gather(prompt, "head", axis=0, tiled=True)

    payload, back = send_queries(
        decode_queries, decode_owner_index, decode_cache_slot, peers, most
    )
    answers = decode_attention(
        payload,
        key_up_weight,
        value_up_weight,
        latent_cache_rows,
        rotated_cache_keys,
        cache_live_lengths,
    )
    decode_out = return_answers(back, answers)
    prompt, _ = lax.optimization_barrier((prompt, answers))
    prompt_attention_output = prefill_attention(
        prompt, query_up_weight, key_up_weight, value_up_weight
    )
    return (prompt_attention_output, decode_out)


def solution(mesh):
    placed = (
        P(("req", "head"), None),
        P(("req", "head"), None),
        P(None, ("req", "head")),
        P(("req", "head")),
        P(None, "head"),
        P(None, "head"),
        P(None, "head"),
        P("req", "head"),
        P("req"),
        P("req"),
        P("req", None, None),
        P("req", None, None),
        P("req"),
    )
    return jax.shard_map(
        on_device,
        mesh=mesh,
        in_specs=placed,
        out_specs=(P("req", "head"), P("req", "head")),
        check_vma=False,
    )
```

```python
import functools
import math

import jax
import jax.numpy as jnp
from jax import lax
from jax.experimental import pallas as pl
from jax.experimental.pallas import tpu as pltpu
from jax.sharding import PartitionSpec as P

D_C = 512
D_NOPE = 128
D_ROPE = 64
D_V = 128
D_Q = D_NOPE + D_ROPE
ROPE_BASE = 10000.0
SCALE = D_Q ** (-0.5)
EXP2_SCALE = SCALE * math.log2(math.e)
MASKED = -1e30
DIGIT = 256
NT = (((1,), (1,)), ((), ()))
TN = (((0,), (0,)), ((), ()))
VMEM_BYTES = 56 * 1024 * 1024


def mm(a, b, dims=(((1,), (0,)), ((), ()))):
    return lax.dot_general(a, b, dims, preferred_element_type=jnp.float32)


def softmax_weights(scores):
    shifted = scores - jnp.max(scores, axis=-1, keepdims=True)
    grown = jnp.exp2(shifted * EXP2_SCALE)
    total = jnp.sum(grown, axis=-1, keepdims=True)
    return (grown * (1.0 / total)).astype(jnp.bfloat16)


def greet(partners):
    barrier = pltpu.get_barrier_semaphore()
    for partner in partners:
        pl.semaphore_signal(
            barrier, inc=1, device_id=partner, device_id_type=pl.DeviceIdType.MESH
        )
    pl.semaphore_wait(barrier, len(partners))


def remote(source, target, send_sem, recv_sem, partner):
    return pltpu.make_async_remote_copy(
        src_ref=source,
        dst_ref=target,
        send_sem=send_sem,
        recv_sem=recv_sem,
        device_id=partner,
        device_id_type=pl.DeviceIdType.MESH,
    )


def peer_at(hop, peers):
    return lax.rem(lax.axis_index("req") + hop, peers)


def exchange_copies(peers, source_ref, target_ref, local_sem, send_sem, recv_sem):
    me = lax.axis_index("req")
    copies = [pltpu.make_async_copy(source_ref.at[me], target_ref.at[me], local_sem)]
    for hop in range(1, peers):
        target = peer_at(hop, peers)
        copies.append(
            remote(
                source_ref.at[target],
                target_ref.at[me],
                send_sem.at[hop],
                recv_sem.at[hop],
                {"req": target},
            )
        )
    return copies


def pack_queries(owner_ref, slot_ref, queries_ref, back_ref, packed_ref):
    peers, most, _ = packed_ref.shape
    rows, width = queries_ref.shape
    owner = owner_ref[...].astype(jnp.float32)
    slot = slot_ref[...].astype(jnp.float32)
    across = jnp.broadcast_to(owner, (rows, rows))
    down = across.T
    before = lax.broadcasted_iota(jnp.int32, (rows, rows), 0) < lax.broadcasted_iota(
        jnp.int32, (rows, rows), 1
    )
    rank = jnp.sum(jnp.where((across == down) & before, 1.0, 0.0), axis=0, keepdims=True)
    place = owner * most + rank
    back_ref[...] = place.astype(jnp.int32)
    index = lax.broadcasted_iota(jnp.int32, (peers * most, rows), 0).astype(jnp.float32)
    placing = index == place
    packed = mm(jnp.where(placing, 1.0, 0.0).astype(jnp.bfloat16), queries_ref[...])
    code = jnp.sum(jnp.where(placing, slot + 1.0, 0.0), axis=1, keepdims=True)
    packed_ref[:, :, :width] = packed.reshape(peers, most, width).astype(jnp.bfloat16)
    packed_ref[:, :, width:] = (
        jnp.broadcast_to(code, (peers * most, 128)).reshape(peers, most, 128).astype(jnp.bfloat16)
    )


def pack_extras(rotary_ref, positions_ref, extras_ref):
    tokens = extras_ref.shape[0]
    rotary = rotary_ref[...].astype(jnp.float32)
    place = jnp.broadcast_to(positions_ref[...].astype(jnp.float32), (D_ROPE, tokens))
    high = jnp.floor(place * (1.0 / DIGIT))
    row = lax.broadcasted_iota(jnp.int32, (D_ROPE, tokens), 0)
    digits = jnp.where(row == 0, high, jnp.where(row == 1, place - high * DIGIT, 0.0))
    extras_ref[...] = jnp.concatenate([rotary, digits], axis=0).T.astype(jnp.bfloat16)


def first_kernel(
    heads,
    owner_ref,
    slot_ref,
    queries_ref,
    latents_in_ref,
    query_latents_in_ref,
    rotary_ref,
    positions_ref,
    frequency_ref,
    query_up_ref,
    key_up_ref,
    value_up_ref,
    payload_ref,
    back_ref,
    query_latents_out_ref,
    latents_out_ref,
    extras_out_ref,
    out_ref,
    packed_ref,
    extras_in_ref,
    query_latents_ref,
    latents_ref,
    extras_ref,
    bias_ref,
    cosine_ref,
    sine_ref,
    key_rope_ref,
    local_sem,
    send_sem,
    recv_sem,
    near_send_sem,
    near_recv_sem,
    keep_sem,
):
    peers = payload_ref.shape[0]
    groups = query_latents_ref.shape[0]
    step = pl.program_id(0)
    group = lax.axis_index("head")
    sibling = group + 1 - 2 * lax.rem(group, 2)
    far = lax.rem(group + groups // 2, groups)
    gathered = (query_latents_ref, latents_ref, extras_ref)
    kept = (query_latents_out_ref, latents_out_ref, extras_out_ref)

    def keeping():
        return [
            pltpu.make_async_copy(source, target, keep_sem.at[index])
            for index, (source, target) in enumerate(zip(gathered, kept))
        ]

    def exchanging():
        return exchange_copies(peers, packed_ref, payload_ref, local_sem, send_sem, recv_sem)

    @pl.when(step == 0)
    def _():
        pack_extras(rotary_ref, positions_ref, extras_in_ref)
        pack_queries(owner_ref, slot_ref, queries_ref, back_ref, packed_ref)
        greet(
            [{"req": peer_at(hop, peers)} for hop in range(1, peers)]
            + [{"head": sibling}, {"head": far}]
        )
        mine = (query_latents_in_ref, latents_in_ref, extras_in_ref)
        near, across, forward = [], [], []
        for index, (source, target) in enumerate(zip(mine, gathered)):
            for kind, (copies, partner) in enumerate(((across, far), (near, sibling))):
                copies.append(
                    remote(
                        source,
                        target.at[group],
                        near_send_sem.at[index, kind],
                        near_recv_sem.at[index, kind],
                        {"head": partner},
                    )
                )
        for copy in across:
            copy.start()
        for copy in near:
            copy.start()
        for copy in exchanging():
            copy.start()
        for source, target in zip(mine, gathered):
            target[group] = source[...]
        for index, (copy, target) in enumerate(zip(across, gathered)):
            copy.wait_recv()
            onward = remote(
                target.at[far],
                target.at[far],
                near_send_sem.at[index, 2],
                near_recv_sem.at[index, 2],
                {"head": sibling},
            )
            onward.start()
            forward.append(onward)
        for copy in across:
            copy.wait_send()
        for copy in near + forward:
            copy.wait()
        for copy in keeping():
            copy.start()
        prefill_setup(
            extras_ref, frequency_ref, bias_ref, cosine_ref, sine_ref, key_rope_ref
        )

    prefill_heads(
        heads,
        query_latents_ref,
        latents_ref,
        query_up_ref,
        key_up_ref,
        value_up_ref,
        out_ref,
        bias_ref,
        cosine_ref,
        sine_ref,
        key_rope_ref,
    )

    @pl.when(step == pl.num_programs(0) - 1)
    def _():
        for copy in keeping() + exchanging():
            copy.wait()


def last_kernel(
    heads,
    back_ref,
    answers_ref,
    query_latents_ref,
    latents_ref,
    extras_ref,
    frequency_ref,
    query_up_ref,
    key_up_ref,
    value_up_ref,
    decoded_ref,
    out_ref,
    landed_ref,
    bias_ref,
    cosine_ref,
    sine_ref,
    key_rope_ref,
    local_sem,
    send_sem,
    recv_sem,
):
    peers, most, width = landed_ref.shape
    step = pl.program_id(0)

    def exchanging():
        return exchange_copies(peers, answers_ref, landed_ref, local_sem, send_sem, recv_sem)

    @pl.when(step == 0)
    def _():
        greet([{"req": peer_at(hop, peers)} for hop in range(1, peers)])
        for copy in exchanging():
            copy.start()
        prefill_setup(
            extras_ref, frequency_ref, bias_ref, cosine_ref, sine_ref, key_rope_ref
        )

    prefill_heads(
        heads,
        query_latents_ref,
        latents_ref,
        query_up_ref,
        key_up_ref,
        value_up_ref,
        out_ref,
        bias_ref,
        cosine_ref,
        sine_ref,
        key_rope_ref,
    )

    @pl.when(step == pl.num_programs(0) - 1)
    def _():
        for copy in exchanging():
            copy.wait()
        blocks = landed_ref[...].astype(jnp.float32).reshape(peers * most, width)
        index = lax.broadcasted_iota(jnp.int32, (peers * most, back_ref.shape[1]), 0)
        wanted = jnp.where(index == back_ref[...], 1.0, 0.0).astype(jnp.bfloat16)
        decoded_ref[...] = mm(wanted, blocks.astype(jnp.bfloat16), TN).astype(jnp.bfloat16)


def exchange_sems(peers):
    return [
        pltpu.SemaphoreType.DMA,
        pltpu.SemaphoreType.DMA((peers,)),
        pltpu.SemaphoreType.DMA((peers,)),
    ]


def decode_kernel(
    slots_per_step,
    head_count,
    lengths_ref,
    payload_ref,
    key_up_ref,
    value_up_ref,
    cache_ref,
    rope_ref,
    out_ref,
    query_ref,
    rope_query_ref,
    latent_out_ref,
):
    step = pl.program_id(0)
    width = head_count * D_Q
    slot_count = query_ref.shape[1] // head_count
    chunks = query_ref.shape[0]
    rows = slots_per_step * head_count
    peers, most, _ = payload_ref.shape
    items = peers * most

    def chosen():
        code = payload_ref[:, :, width:].astype(jnp.float32).reshape(items, 128)[:, :1]
        slots = lax.broadcasted_iota(jnp.int32, (items, slot_count), 1).astype(jnp.float32)
        return jnp.where(code == slots + 1.0, 1.0, 0.0).astype(jnp.bfloat16)

    @pl.when(step == 0)
    def _():
        received = payload_ref[:, :, :width].reshape(items, width)
        queries = mm(chosen(), received, TN)
        for head in range(head_count):
            nope = queries[:, head * D_Q : head * D_Q + D_NOPE].astype(jnp.bfloat16)
            latent = mm(nope, key_up_ref[:, head * D_NOPE : (head + 1) * D_NOPE], NT)
            place = pl.ds(head, slot_count, stride=head_count)
            latent = latent.astype(jnp.bfloat16).astype(jnp.float32)
            for chunk in range(chunks):
                query_ref[chunk, place, :] = latent[:, chunk * 128 : (chunk + 1) * 128]
            rope = queries[:, head * D_Q + D_NOPE : (head + 1) * D_Q]
            rope_query_ref[place, :] = jnp.concatenate([rope, rope], axis=1)

    first = pl.multiple_of(step * slots_per_step, slots_per_step)
    here = pl.ds(pl.multiple_of(step * rows, rows), rows)
    columns = jnp.concatenate(
        [query_ref[chunk, here, :].T for chunk in range(chunks)], axis=0
    ).astype(jnp.bfloat16)
    rope_query = rope_query_ref[here, :D_ROPE].astype(jnp.bfloat16)
    owner = lax.broadcasted_iota(jnp.int32, columns.shape, 1) // head_count
    none = jnp.zeros_like(columns)
    turned = None
    for item in range(slots_per_step):
        part = mm(cache_ref[item], jnp.where(owner == item, columns, none))
        turned = part if turned is None else turned + part
    scores = turned.T
    lanes = lax.broadcasted_iota(jnp.int32, (head_count, cache_ref.shape[1]), 1)
    parts = []
    for item in range(slots_per_step):
        place = slice(item * head_count, (item + 1) * head_count)
        part = scores[place] + mm(rope_query[place], rope_ref[item])
        parts.append(jnp.where(lanes < lengths_ref[first + item], part, MASKED))
    weights = softmax_weights(jnp.concatenate(parts, axis=0))
    for item in range(slots_per_step):
        place = slice(item * head_count, (item + 1) * head_count)
        latent = mm(weights[place], cache_ref[item]).astype(jnp.bfloat16).astype(jnp.float32)
        below = pl.ds(pl.multiple_of(step * rows, rows) + item * head_count, head_count)
        for chunk in range(chunks):
            latent_out_ref[chunk, below, :] = latent[:, chunk * 128 : (chunk + 1) * 128]

    @pl.when(step == pl.num_programs(0) - 1)
    def _():
        sending = chosen()
        for head in range(head_count):
            strided = pl.ds(head, slot_count, stride=head_count)
            latent = jnp.concatenate(
                [latent_out_ref[chunk, strided, :] for chunk in range(chunks)], axis=1
            )
            place = slice(head * D_V, (head + 1) * D_V)
            answer = mm(latent.astype(jnp.bfloat16), value_up_ref[:, place])
            answer = mm(sending, answer.astype(jnp.bfloat16)).astype(jnp.bfloat16)
            out_ref[:, :, place] = answer.reshape(peers, most, D_V)


def decode_attention(payload, key_up, value_up, cache, rope_cache, lengths):
    slot_count, cache_rows, _ = cache.shape
    head_count = key_up.shape[1] // D_NOPE
    per_step = 8
    peers, most, _ = payload.shape
    whole = lambda step, *_: (0, 0)
    single = lambda step, *_: (0, 0, 0)
    flops = 2 * slot_count * head_count * (2 * D_NOPE * D_C + 17 * cache_rows * D_C)
    block = jax.ShapeDtypeStruct((peers, most, head_count * D_V), jnp.bfloat16)
    return pl.pallas_call(
        functools.partial(decode_kernel, per_step, head_count),
        out_shape=block,
        grid_spec=pltpu.PrefetchScalarGridSpec(
            num_scalar_prefetch=1,
            grid=(slot_count // per_step,),
            in_specs=[
                pl.BlockSpec(payload.shape, single),
                pl.BlockSpec(key_up.shape, whole),
                pl.BlockSpec(value_up.shape, whole),
                pl.BlockSpec((per_step, cache_rows, D_C), lambda step, *_: (step, 0, 0)),
                pl.BlockSpec((per_step, D_ROPE, cache_rows), lambda step, *_: (step, 0, 0)),
            ],
            out_specs=pl.BlockSpec(block.shape, single),
            scratch_shapes=[
                pltpu.VMEM((D_C // 128, slot_count * head_count, 128), jnp.float32),
                pltpu.VMEM((slot_count * head_count, 2 * D_ROPE), jnp.float32),
                pltpu.VMEM((D_C // 128, slot_count * head_count, 128), jnp.float32),
            ],
        ),
        compiler_params=pltpu.CompilerParams(vmem_limit_bytes=VMEM_BYTES),
        cost_estimate=pl.CostEstimate(
            flops=flops, bytes_accessed=cache.size * 2 + payload.size * 2, transcendentals=0
        ),
    )(lengths, payload, key_up, value_up, cache, rope_cache)


def lane_marks(tokens):
    lanes = lax.broadcasted_iota(jnp.int32, (tokens, D_NOPE), 1)
    return lanes < D_ROPE, lanes % D_ROPE < D_ROPE // 2


def rotated(values, leading, cosine_ref, sine_ref):
    swapped = jnp.where(
        leading,
        pltpu.roll(values, D_NOPE - D_ROPE // 2, 1),
        pltpu.roll(values, D_ROPE // 2, 1),
    )
    return values * cosine_ref[...] + swapped * sine_ref[...]


def prefill_setup(extras_ref, frequency_ref, bias_ref, cosine_ref, sine_ref, key_rope_ref):
    tokens = bias_ref.shape[0]
    low, leading = lane_marks(tokens)
    extras = extras_ref[...].astype(jnp.float32).reshape(tokens, D_NOPE)
    position = extras[:, D_ROPE : D_ROPE + 1] * DIGIT + extras[:, D_ROPE + 1 : D_ROPE + 2]
    row = lax.broadcasted_iota(jnp.int32, (tokens, tokens), 0).astype(jnp.float32)
    column = lax.broadcasted_iota(jnp.int32, (tokens, tokens), 1).astype(jnp.float32)
    visible = (column <= row) & (column >= row - position)
    bias_ref[...] = jnp.where(visible, 0.0, MASKED)
    angles = position * frequency_ref[...]
    cosine_ref[...] = jnp.cos(angles)
    sines = jnp.sin(angles)
    sine_ref[...] = jnp.where(leading, -sines, sines)
    twice = jnp.where(low, extras, pltpu.roll(extras, D_ROPE, 1))
    turned = rotated(twice, leading, cosine_ref, sine_ref)
    key_rope_ref[...] = turned.T[:D_ROPE].astype(jnp.bfloat16)


def prefill_heads(
    heads,
    query_latents_ref,
    latents_ref,
    query_up_ref,
    key_up_ref,
    value_up_ref,
    out_ref,
    bias_ref,
    cosine_ref,
    sine_ref,
    key_rope_ref,
):
    tokens = bias_ref.shape[0]
    low, leading = lane_marks(tokens)
    query_latents = query_latents_ref[...].reshape(tokens, query_up_ref.shape[0])
    latents = latents_ref[...].reshape(tokens, key_up_ref.shape[0])
    projected = mm(query_latents, query_up_ref[...])
    keys = mm(latents, key_up_ref[...]).astype(jnp.bfloat16).T
    values = mm(latents, value_up_ref[...]).astype(jnp.bfloat16)
    key_rope = key_rope_ref[...]
    none = jnp.zeros((D_ROPE, tokens), jnp.bfloat16)
    tile = min(256, tokens)
    work = []
    for pair in range(heads // 2):
        base = pair * 2 * D_Q
        left = projected[:, base : base + D_NOPE].astype(jnp.bfloat16)
        middle = projected[:, base + D_NOPE : base + 2 * D_NOPE]
        middle = jnp.where(low, rotated(middle, leading, cosine_ref, sine_ref), middle).astype(jnp.bfloat16)
        right = projected[:, base + 2 * D_NOPE : base + 3 * D_NOPE]
        right = jnp.where(low, right, rotated(right, leading, cosine_ref, sine_ref)).astype(jnp.bfloat16)
        even = keys[2 * pair * D_NOPE : (2 * pair + 1) * D_NOPE]
        odd = keys[(2 * pair + 1) * D_NOPE : (2 * pair + 2) * D_NOPE]
        both = (
            (
                jnp.concatenate([left, middle], axis=1),
                jnp.concatenate([even, key_rope, none], axis=0),
            ),
            (
                jnp.concatenate([middle, right], axis=1),
                jnp.concatenate([none, odd, key_rope], axis=0),
            ),
        )
        for side, (query, key) in enumerate(both):
            place = slice((2 * pair + side) * D_V, (2 * pair + side + 1) * D_V)
            for begin in range(0, tokens, tile):
                work.append((query, key, place, begin, begin + tile))

    def score(query, key, place, begin, end):
        return mm(query[begin:end], key[:, :end]) + bias_ref[begin:end, :end]

    scores = score(*work[0])
    for index, (_, _, place, begin, end) in enumerate(work):
        following = score(*work[index + 1]) if index + 1 < len(work) else None
        weights = softmax_weights(scores)
        out_ref[begin:end, place] = mm(weights, values[:end, place]).astype(jnp.bfloat16)
        scores = following


def prefill_scratch(tokens):
    return [
        pltpu.VMEM((tokens, tokens), jnp.float32),
        pltpu.VMEM((tokens, D_NOPE), jnp.float32),
        pltpu.VMEM((tokens, D_NOPE), jnp.float32),
        pltpu.VMEM((D_ROPE, tokens), jnp.bfloat16),
    ]


def weight_specs(heads, start, query_latent_width):
    across = lambda step: (0, step + start)
    return [
        pl.BlockSpec((query_latent_width, heads * D_Q), across),
        pl.BlockSpec((D_C, heads * D_NOPE), across),
        pl.BlockSpec((D_C, heads * D_V), across),
    ]


def first_call(
    owner, slot, queries, latents, query_latents, rotary, positions, frequency, weights, split, most
):
    peers, groups = lax.axis_size("req"), lax.axis_size("head")
    heads, steps, _ = split
    rows, width = queries.shape
    part, query_latent_width = query_latents.shape
    tokens = part * groups
    vmem = pl.BlockSpec(memory_space=pltpu.VMEM)
    remote_space = pl.BlockSpec(memory_space=pl.ANY)
    packed = (peers, most, width + 128)
    gathered = [
        (groups, part, query_latent_width),
        (groups, part, D_C),
        (groups, part, D_NOPE),
    ]
    return pl.pallas_call(
        functools.partial(first_kernel, heads),
        out_shape=(
            jax.ShapeDtypeStruct(packed, jnp.bfloat16),
            jax.ShapeDtypeStruct((1, rows), jnp.int32),
            *(jax.ShapeDtypeStruct(shape, jnp.bfloat16) for shape in gathered),
            jax.ShapeDtypeStruct((tokens, steps * heads * D_V), jnp.bfloat16),
        ),
        grid=(steps,),
        in_specs=[vmem] * 8 + weight_specs(heads, 0, query_latent_width),
        out_specs=(
            remote_space,
            vmem,
            remote_space,
            remote_space,
            remote_space,
            pl.BlockSpec((tokens, heads * D_V), lambda step: (0, step)),
        ),
        scratch_shapes=[
            pltpu.VMEM(packed, jnp.bfloat16),
            pltpu.VMEM((part, D_NOPE), jnp.bfloat16),
            *(pltpu.VMEM(shape, jnp.bfloat16) for shape in gathered),
            *prefill_scratch(tokens),
            *exchange_sems(peers),
            pltpu.SemaphoreType.DMA((3, 3)),
            pltpu.SemaphoreType.DMA((3, 3)),
            pltpu.SemaphoreType.DMA((3,)),
        ],
        compiler_params=pltpu.CompilerParams(
            vmem_limit_bytes=VMEM_BYTES, collective_id=0, has_side_effects=True
        ),
    )(
        owner[None, :],
        slot[None, :],
        queries,
        latents,
        query_latents,
        rotary,
        positions[None, :],
        frequency,
        *weights,
    )


def last_call(back, answers, gathered, frequency, weights, split):
    peers = answers.shape[0]
    heads, steps, start = split
    groups, part, query_latent_width = gathered[0].shape
    tokens = groups * part
    vmem = pl.BlockSpec(memory_space=pltpu.VMEM)
    return pl.pallas_call(
        functools.partial(last_kernel, heads),
        out_shape=(
            jax.ShapeDtypeStruct((back.shape[1], answers.shape[2]), jnp.bfloat16),
            jax.ShapeDtypeStruct((tokens, steps * heads * D_V), jnp.bfloat16),
        ),
        grid=(steps,),
        in_specs=[vmem, pl.BlockSpec(memory_space=pl.ANY)]
        + [vmem] * 4
        + weight_specs(heads, start, query_latent_width),
        out_specs=(vmem, pl.BlockSpec((tokens, heads * D_V), lambda step: (0, step))),
        scratch_shapes=[
            pltpu.VMEM(answers.shape, jnp.bfloat16),
            *prefill_scratch(tokens),
            *exchange_sems(peers),
        ],
        compiler_params=pltpu.CompilerParams(
            vmem_limit_bytes=VMEM_BYTES, collective_id=1, has_side_effects=True
        ),
    )(back, answers, *gathered, frequency, *weights)


def on_device(
    prompt_query_latents,
    prompt_latents,
    prompt_rotary_keys,
    positions,
    query_up_weight,
    key_up_weight,
    value_up_weight,
    decode_queries,
    decode_owner_index,
    decode_cache_slot,
    latent_cache_rows,
    rotated_cache_keys,
    cache_live_lengths,
):
    row_count = decode_queries.shape[0]
    peers = lax.axis_size("req")
    most = max(2, row_count * 2 // peers)
    half_width = D_ROPE // 2
    frequency = ROPE_BASE ** (-jnp.arange(half_width, dtype=jnp.float32) / half_width)
    frequency = jnp.tile(frequency, 4)[None, :]
    weights = (query_up_weight, key_up_weight, value_up_weight)
    head_count = key_up_weight.shape[1] // D_NOPE
    heads = 4
    steps = head_count // heads
    early = steps // 2

    payload, back, *gathered, first_half = first_call(
        decode_owner_index,
        decode_cache_slot,
        decode_queries,
        prompt_latents,
        prompt_query_latents,
        prompt_rotary_keys,
        positions,
        frequency,
        weights,
        (heads, early, 0),
        most,
    )
    answers = decode_attention(
        payload,
        key_up_weight,
        value_up_weight,
        latent_cache_rows,
        rotated_cache_keys,
        cache_live_lengths,
    )
    decode_out, second_half = last_call(
        back, answers, gathered, frequency, weights, (heads, steps - early, early)
    )
    return (jnp.concatenate([first_half, second_half], axis=1), decode_out)


def solution(mesh):
    placed = (
        P(("req", "head"), None),
        P(("req", "head"), None),
        P(None, ("req", "head")),
        P(("req", "head")),
        P(None, "head"),
        P(None, "head"),
        P(None, "head"),
        P("req", "head"),
        P("req"),
        P("req"),
        P("req", None, None),
        P("req", None, None),
        P("req"),
    )
    return jax.shard_map(
        on_device,
        mesh=mesh,
        in_specs=placed,
        out_specs=(P("req", "head"), P("req", "head")),
        check_vma=False,
    )
```

```python
import functools
import math

import jax
import jax.numpy as jnp
from jax import lax
from jax.experimental import pallas as pl
from jax.experimental.pallas import tpu as pltpu
from jax.sharding import PartitionSpec as P

D_C = 512
D_NOPE = 128
D_ROPE = 64
D_V = 128
D_Q = D_NOPE + D_ROPE
ROPE_BASE = 10000.0
SCALE = D_Q ** (-0.5)
EXP2_SCALE = SCALE * math.log2(math.e)
MASKED = -1e30
DIGIT = 256
NT = (((1,), (1,)), ((), ()))
TN = (((0,), (0,)), ((), ()))
VMEM_BYTES = 40 * 1024 * 1024


def mm(a, b, dims=(((1,), (0,)), ((), ()))):
    return lax.dot_general(a, b, dims, preferred_element_type=jnp.float32)


def softmax_weights(scores):
    shifted = scores - jnp.max(scores, axis=-1, keepdims=True)
    grown = jnp.exp2(shifted * EXP2_SCALE)
    total = jnp.sum(grown, axis=-1, keepdims=True)
    return (grown * (1.0 / total)).astype(jnp.bfloat16)


def greet(partners):
    barrier = pltpu.get_barrier_semaphore()
    for partner in partners:
        pl.semaphore_signal(
            barrier, inc=1, device_id=partner, device_id_type=pl.DeviceIdType.MESH
        )
    pl.semaphore_wait(barrier, len(partners))


def remote(source, target, send_sem, recv_sem, partner):
    return pltpu.make_async_remote_copy(
        src_ref=source,
        dst_ref=target,
        send_sem=send_sem,
        recv_sem=recv_sem,
        device_id=partner,
        device_id_type=pl.DeviceIdType.MESH,
    )


def peer_at(hop, peers):
    return lax.rem(lax.axis_index("req") + hop, peers)


def exchange_copies(peers, source_ref, target_ref, local_sem, send_sem, recv_sem):
    me = lax.axis_index("req")
    copies = [pltpu.make_async_copy(source_ref.at[me], target_ref.at[me], local_sem)]
    for hop in range(1, peers):
        target = peer_at(hop, peers)
        copies.append(
            remote(
                source_ref.at[target],
                target_ref.at[me],
                send_sem.at[hop],
                recv_sem.at[hop],
                {"req": target},
            )
        )
    return copies


def pack_queries(owner_ref, slot_ref, queries_ref, back_ref, packed_ref):
    peers, most, _ = packed_ref.shape
    rows, width = queries_ref.shape
    owner = owner_ref[...].astype(jnp.float32)
    slot = slot_ref[...].astype(jnp.float32)
    across = jnp.broadcast_to(owner, (rows, rows))
    down = across.T
    before = lax.broadcasted_iota(jnp.int32, (rows, rows), 0) < lax.broadcasted_iota(
        jnp.int32, (rows, rows), 1
    )
    rank = jnp.sum(jnp.where((across == down) & before, 1.0, 0.0), axis=0, keepdims=True)
    place = owner * most + rank
    back_ref[...] = place.astype(jnp.int32)
    index = lax.broadcasted_iota(jnp.int32, (peers * most, rows), 0).astype(jnp.float32)
    placing = index == place
    packed = mm(jnp.where(placing, 1.0, 0.0).astype(jnp.bfloat16), queries_ref[...])
    code = jnp.sum(jnp.where(placing, slot + 1.0, 0.0), axis=1, keepdims=True)
    packed_ref[:, :, :width] = packed.reshape(peers, most, width).astype(jnp.bfloat16)
    packed_ref[:, :, width:] = (
        jnp.broadcast_to(code, (peers * most, 128)).reshape(peers, most, 128).astype(jnp.bfloat16)
    )


def pack_extras(rotary_ref, positions_ref, extras_ref):
    tokens = extras_ref.shape[0]
    rotary = rotary_ref[...].astype(jnp.float32)
    place = jnp.broadcast_to(positions_ref[...].astype(jnp.float32), (D_ROPE, tokens))
    high = jnp.floor(place * (1.0 / DIGIT))
    row = lax.broadcasted_iota(jnp.int32, (D_ROPE, tokens), 0)
    digits = jnp.where(row == 0, high, jnp.where(row == 1, place - high * DIGIT, 0.0))
    extras_ref[...] = jnp.concatenate([rotary, digits], axis=0).T.astype(jnp.bfloat16)


def first_kernel(
    heads,
    owner_ref,
    slot_ref,
    queries_ref,
    latents_in_ref,
    query_latents_in_ref,
    rotary_ref,
    positions_ref,
    frequency_ref,
    query_up_ref,
    key_up_ref,
    value_up_ref,
    payload_ref,
    back_ref,
    query_latents_out_ref,
    latents_out_ref,
    extras_out_ref,
    out_ref,
    packed_ref,
    extras_in_ref,
    query_latents_ref,
    latents_ref,
    extras_ref,
    bias_ref,
    cosine_ref,
    sine_ref,
    key_rope_ref,
    local_sem,
    send_sem,
    recv_sem,
    near_send_sem,
    near_recv_sem,
    keep_sem,
):
    peers = payload_ref.shape[0]
    groups = query_latents_ref.shape[0]
    step = pl.program_id(0)
    group = lax.axis_index("head")
    sibling = group + 1 - 2 * lax.rem(group, 2)
    far = lax.rem(group + groups // 2, groups)
    gathered = (query_latents_ref, latents_ref, extras_ref)
    kept = (query_latents_out_ref, latents_out_ref, extras_out_ref)

    def keeping():
        return [
            pltpu.make_async_copy(source, target, keep_sem.at[index])
            for index, (source, target) in enumerate(zip(gathered, kept))
        ]

    def exchanging():
        return exchange_copies(peers, packed_ref, payload_ref, local_sem, send_sem, recv_sem)

    @pl.when(step == 0)
    def _():
        pack_extras(rotary_ref, positions_ref, extras_in_ref)
        pack_queries(owner_ref, slot_ref, queries_ref, back_ref, packed_ref)
        greet(
            [{"req": peer_at(hop, peers)} for hop in range(1, peers)]
            + [{"head": sibling}, {"head": far}]
        )
        mine = (query_latents_in_ref, latents_in_ref, extras_in_ref)
        near, across = [], []
        for index, (source, target) in enumerate(zip(mine, gathered)):
            for kind, (copies, partner) in enumerate(((across, far), (near, sibling))):
                copies.append(
                    remote(
                        source,
                        target.at[group],
                        near_send_sem.at[index, kind],
                        near_recv_sem.at[index, kind],
                        {"head": partner},
                    )
                )
        for copy in across[::-1]:
            copy.start()
        for copy in near[::-1]:
            copy.start()
        for copy in exchanging():
            copy.start()
        for source, target in zip(mine, gathered):
            target[group] = source[...]

        def pass_on(index):
            target = gathered[index]
            across[index].wait_recv()
            onward = remote(
                target.at[far],
                target.at[far],
                near_send_sem.at[index, 2],
                near_recv_sem.at[index, 2],
                {"head": sibling},
            )
            onward.start()
            return onward

        forward = pass_on(2)
        near[2].wait()
        forward.wait()
        prefill_setup(
            extras_ref, frequency_ref, bias_ref, cosine_ref, sine_ref, key_rope_ref
        )
        forward = [pass_on(1), pass_on(0)]
        for copy in across:
            copy.wait_send()
        for copy in near[:2] + forward:
            copy.wait()
        for copy in keeping():
            copy.start()

    prefill_heads(
        heads,
        query_latents_ref,
        latents_ref,
        query_up_ref,
        key_up_ref,
        value_up_ref,
        out_ref,
        bias_ref,
        cosine_ref,
        sine_ref,
        key_rope_ref,
    )

    @pl.when(step == pl.num_programs(0) - 1)
    def _():
        for copy in keeping() + exchanging():
            copy.wait()


def last_kernel(
    heads,
    back_ref,
    answers_ref,
    query_latents_ref,
    latents_ref,
    extras_ref,
    frequency_ref,
    query_up_ref,
    key_up_ref,
    value_up_ref,
    decoded_ref,
    out_ref,
    landed_ref,
    bias_ref,
    cosine_ref,
    sine_ref,
    key_rope_ref,
    local_sem,
    send_sem,
    recv_sem,
):
    peers, most, width = landed_ref.shape
    step = pl.program_id(0)

    def exchanging():
        return exchange_copies(peers, answers_ref, landed_ref, local_sem, send_sem, recv_sem)

    @pl.when(step == 0)
    def _():
        greet([{"req": peer_at(hop, peers)} for hop in range(1, peers)])
        for copy in exchanging():
            copy.start()
        prefill_setup(
            extras_ref, frequency_ref, bias_ref, cosine_ref, sine_ref, key_rope_ref
        )

    prefill_heads(
        heads,
        query_latents_ref,
        latents_ref,
        query_up_ref,
        key_up_ref,
        value_up_ref,
        out_ref,
        bias_ref,
        cosine_ref,
        sine_ref,
        key_rope_ref,
    )

    @pl.when(step == pl.num_programs(0) - 1)
    def _():
        for copy in exchanging():
            copy.wait()
        blocks = landed_ref[...].astype(jnp.float32).reshape(peers * most, width)
        index = lax.broadcasted_iota(jnp.int32, (peers * most, back_ref.shape[1]), 0)
        wanted = jnp.where(index == back_ref[...], 1.0, 0.0).astype(jnp.bfloat16)
        decoded_ref[...] = mm(wanted, blocks.astype(jnp.bfloat16), TN).astype(jnp.bfloat16)


def exchange_sems(peers):
    return [
        pltpu.SemaphoreType.DMA,
        pltpu.SemaphoreType.DMA((peers,)),
        pltpu.SemaphoreType.DMA((peers,)),
    ]


def decode_kernel(
    slots_per_step,
    head_count,
    lengths_ref,
    payload_ref,
    key_up_ref,
    value_up_ref,
    cache_ref,
    rope_ref,
    out_ref,
    query_ref,
    rope_query_ref,
    latent_out_ref,
    value_ref,
):
    step = pl.program_id(0)
    value_width = value_up_ref.shape[1]
    value_ref[:, pl.ds(pl.multiple_of(step * value_width, value_width), value_width)] = (
        value_up_ref[...]
    )
    width = head_count * D_Q
    slot_count = query_ref.shape[1] // head_count
    chunks = query_ref.shape[0]
    rows = slots_per_step * head_count
    peers, most, _ = payload_ref.shape
    items = peers * most

    def chosen():
        code = payload_ref[:, :, width:].astype(jnp.float32).reshape(items, 128)[:, :1]
        slots = lax.broadcasted_iota(jnp.int32, (items, slot_count), 1).astype(jnp.float32)
        return jnp.where(code == slots + 1.0, 1.0, 0.0).astype(jnp.bfloat16)

    @pl.when(step == 0)
    def _():
        received = payload_ref[:, :, :width].reshape(items, width)
        queries = mm(chosen(), received, TN)
        for head in range(head_count):
            nope = queries[:, head * D_Q : head * D_Q + D_NOPE].astype(jnp.bfloat16)
            latent = mm(nope, key_up_ref[:, head * D_NOPE : (head + 1) * D_NOPE], NT)
            place = pl.ds(head, slot_count, stride=head_count)
            latent = latent.astype(jnp.bfloat16).astype(jnp.float32)
            for chunk in range(chunks):
                query_ref[chunk, place, :] = latent[:, chunk * 128 : (chunk + 1) * 128]
            rope = queries[:, head * D_Q + D_NOPE : (head + 1) * D_Q]
            rope_query_ref[place, :] = jnp.concatenate([rope, rope], axis=1)

    first = step * slots_per_step
    unit = 128 // head_count
    cache_rows = cache_ref.shape[1]
    lanes = lax.broadcasted_iota(jnp.int32, (head_count, cache_rows), 1)
    owner = lax.broadcasted_iota(jnp.int32, (cache_rows, 128), 1) // head_count
    batches = range(0, slots_per_step, unit)
    products = []
    for batch in batches:
        here = pl.ds(pl.multiple_of(step * rows, 128) + batch * head_count, 128)
        columns = jnp.concatenate(
            [query_ref[chunk, here, :].T for chunk in range(chunks)], axis=0
        ).astype(jnp.bfloat16)
        latents = cache_ref[batch : batch + unit].reshape(unit * cache_rows, D_C)
        products.append(mm(latents, columns))
    for batch, product in zip(batches, products):
        here = pl.ds(pl.multiple_of(step * rows, 128) + batch * head_count, 128)
        turned = product[:cache_rows]
        for item in range(1, unit):
            place = slice(item * cache_rows, (item + 1) * cache_rows)
            turned = jnp.where(owner == item, product[place], turned)
        scores = turned.T
        rope_query = rope_query_ref[here, :D_ROPE].astype(jnp.bfloat16)
        parts = []
        for item in range(unit):
            place = slice(item * head_count, (item + 1) * head_count)
            part = scores[place] + mm(rope_query[place], rope_ref[batch + item])
            parts.append(jnp.where(lanes < lengths_ref[first + batch + item], part, MASKED))
        weights = softmax_weights(jnp.concatenate(parts, axis=0))
        latent = jnp.concatenate(
            [
                mm(weights[item * head_count : (item + 1) * head_count], cache_ref[batch + item])
                for item in range(unit)
            ],
            axis=0,
        )
        latent = latent.astype(jnp.bfloat16).astype(jnp.float32)
        for chunk in range(chunks):
            latent_out_ref[chunk, here, :] = latent[:, chunk * 128 : (chunk + 1) * 128]

    @pl.when(step == pl.num_programs(0) - 1)
    def _():
        sending = chosen()
        for head in range(head_count):
            strided = pl.ds(head, slot_count, stride=head_count)
            latent = jnp.concatenate(
                [latent_out_ref[chunk, strided, :] for chunk in range(chunks)], axis=1
            )
            place = slice(head * D_V, (head + 1) * D_V)
            answer = mm(latent.astype(jnp.bfloat16), value_ref[:, place])
            answer = mm(sending, answer.astype(jnp.bfloat16)).astype(jnp.bfloat16)
            out_ref[:, :, place] = answer.reshape(peers, most, D_V)


def decode_attention(payload, key_up, value_up, cache, rope_cache, lengths):
    slot_count, cache_rows, _ = cache.shape
    head_count = key_up.shape[1] // D_NOPE
    per_step = 16
    steps = slot_count // per_step
    peers, most, _ = payload.shape
    whole = lambda step, *_: (0, 0)
    single = lambda step, *_: (0, 0, 0)
    flops = 2 * slot_count * head_count * (2 * D_NOPE * D_C + 17 * cache_rows * D_C)
    block = jax.ShapeDtypeStruct((peers, most, head_count * D_V), jnp.bfloat16)
    return pl.pallas_call(
        functools.partial(decode_kernel, per_step, head_count),
        out_shape=block,
        grid_spec=pltpu.PrefetchScalarGridSpec(
            num_scalar_prefetch=1,
            grid=(steps,),
            in_specs=[
                pl.BlockSpec(payload.shape, single),
                pl.BlockSpec(key_up.shape, whole),
                pl.BlockSpec((D_C, value_up.shape[1] // steps), lambda step, *_: (0, step)),
                pl.BlockSpec((per_step, cache_rows, D_C), lambda step, *_: (step, 0, 0)),
                pl.BlockSpec((per_step, D_ROPE, cache_rows), lambda step, *_: (step, 0, 0)),
            ],
            out_specs=pl.BlockSpec(block.shape, single),
            scratch_shapes=[
                pltpu.VMEM((D_C // 128, slot_count * head_count, 128), jnp.float32),
                pltpu.VMEM((slot_count * head_count, 2 * D_ROPE), jnp.float32),
                pltpu.VMEM((D_C // 128, slot_count * head_count, 128), jnp.float32),
                pltpu.VMEM(value_up.shape, jnp.bfloat16),
            ],
        ),
        compiler_params=pltpu.CompilerParams(vmem_limit_bytes=VMEM_BYTES),
        cost_estimate=pl.CostEstimate(
            flops=flops, bytes_accessed=cache.size * 2 + payload.size * 2, transcendentals=0
        ),
    )(lengths, payload, key_up, value_up, cache, rope_cache)


def lane_marks(tokens):
    lanes = lax.broadcasted_iota(jnp.int32, (tokens, D_NOPE), 1)
    return lanes < D_ROPE, lanes % D_ROPE < D_ROPE // 2


def rotated(values, leading, cosine_ref, sine_ref):
    swapped = jnp.where(
        leading,
        pltpu.roll(values, D_NOPE - D_ROPE // 2, 1),
        pltpu.roll(values, D_ROPE // 2, 1),
    )
    return values * cosine_ref[...] + swapped * sine_ref[...]


def prefill_setup(extras_ref, frequency_ref, bias_ref, cosine_ref, sine_ref, key_rope_ref):
    tokens = bias_ref.shape[0]
    low, leading = lane_marks(tokens)
    extras = extras_ref[...].astype(jnp.float32).reshape(tokens, D_NOPE)
    position = extras[:, D_ROPE : D_ROPE + 1] * DIGIT + extras[:, D_ROPE + 1 : D_ROPE + 2]
    row = lax.broadcasted_iota(jnp.int32, (tokens, tokens), 0).astype(jnp.float32)
    column = lax.broadcasted_iota(jnp.int32, (tokens, tokens), 1).astype(jnp.float32)
    visible = (column <= row) & (column >= row - position)
    bias_ref[...] = jnp.where(visible, 0.0, MASKED)
    angles = position * frequency_ref[...]
    cosine_ref[...] = jnp.cos(angles)
    sines = jnp.sin(angles)
    sine_ref[...] = jnp.where(leading, -sines, sines)
    twice = jnp.where(low, extras, pltpu.roll(extras, D_ROPE, 1))
    turned = rotated(twice, leading, cosine_ref, sine_ref)
    key_rope_ref[...] = turned.T[:D_ROPE].astype(jnp.bfloat16)


def prefill_heads(
    heads,
    query_latents_ref,
    latents_ref,
    query_up_ref,
    key_up_ref,
    value_up_ref,
    out_ref,
    bias_ref,
    cosine_ref,
    sine_ref,
    key_rope_ref,
):
    tokens = bias_ref.shape[0]
    low, leading = lane_marks(tokens)
    query_latents = query_latents_ref[...].reshape(tokens, query_up_ref.shape[0])
    latents = latents_ref[...].reshape(tokens, key_up_ref.shape[0])
    projected = mm(query_latents, query_up_ref[...])
    keys = mm(latents, key_up_ref[...]).astype(jnp.bfloat16).T
    values = mm(latents, value_up_ref[...]).astype(jnp.bfloat16)
    key_rope = key_rope_ref[...]
    none = jnp.zeros((D_ROPE, tokens), jnp.bfloat16)
    tile = min(256, tokens)
    work = []
    for pair in range(heads // 2):
        base = pair * 2 * D_Q
        left = projected[:, base : base + D_NOPE].astype(jnp.bfloat16)
        middle = projected[:, base + D_NOPE : base + 2 * D_NOPE]
        middle = jnp.where(low, rotated(middle, leading, cosine_ref, sine_ref), middle).astype(jnp.bfloat16)
        right = projected[:, base + 2 * D_NOPE : base + 3 * D_NOPE]
        right = jnp.where(low, right, rotated(right, leading, cosine_ref, sine_ref)).astype(jnp.bfloat16)
        even = keys[2 * pair * D_NOPE : (2 * pair + 1) * D_NOPE]
        odd = keys[(2 * pair + 1) * D_NOPE : (2 * pair + 2) * D_NOPE]
        both = (
            (
                jnp.concatenate([left, middle], axis=1),
                jnp.concatenate([even, key_rope, none], axis=0),
            ),
            (
                jnp.concatenate([middle, right], axis=1),
                jnp.concatenate([none, odd, key_rope], axis=0),
            ),
        )
        for side, (query, key) in enumerate(both):
            place = slice((2 * pair + side) * D_V, (2 * pair + side + 1) * D_V)
            for begin in range(0, tokens, tile):
                work.append((query, key, place, begin, begin + tile))

    def score(query, key, place, begin, end):
        return mm(query[begin:end], key[:, :end]) + bias_ref[begin:end, :end]

    scores = score(*work[0])
    for index, (_, _, place, begin, end) in enumerate(work):
        following = score(*work[index + 1]) if index + 1 < len(work) else None
        weights = softmax_weights(scores)
        out_ref[begin:end, place] = mm(weights, values[:end, place]).astype(jnp.bfloat16)
        scores = following


def prefill_scratch(tokens):
    return [
        pltpu.VMEM((tokens, tokens), jnp.float32),
        pltpu.VMEM((tokens, D_NOPE), jnp.float32),
        pltpu.VMEM((tokens, D_NOPE), jnp.float32),
        pltpu.VMEM((D_ROPE, tokens), jnp.bfloat16),
    ]


def weight_specs(heads, start, query_latent_width):
    across = lambda step: (0, step + start)
    return [
        pl.BlockSpec((query_latent_width, heads * D_Q), across),
        pl.BlockSpec((D_C, heads * D_NOPE), across),
        pl.BlockSpec((D_C, heads * D_V), across),
    ]


def first_call(
    owner, slot, queries, latents, query_latents, rotary, positions, frequency, weights, split, most
):
    peers, groups = lax.axis_size("req"), lax.axis_size("head")
    heads, steps, _ = split
    rows, width = queries.shape
    part, query_latent_width = query_latents.shape
    tokens = part * groups
    vmem = pl.BlockSpec(memory_space=pltpu.VMEM)
    remote_space = pl.BlockSpec(memory_space=pl.ANY)
    packed = (peers, most, width + 128)
    gathered = [
        (groups, part, query_latent_width),
        (groups, part, D_C),
        (groups, part, D_NOPE),
    ]
    return pl.pallas_call(
        functools.partial(first_kernel, heads),
        out_shape=(
            jax.ShapeDtypeStruct(packed, jnp.bfloat16),
            jax.ShapeDtypeStruct((1, rows), jnp.int32),
            *(jax.ShapeDtypeStruct(shape, jnp.bfloat16) for shape in gathered),
            jax.ShapeDtypeStruct((tokens, steps * heads * D_V), jnp.bfloat16),
        ),
        grid=(steps,),
        in_specs=[vmem] * 8 + weight_specs(heads, 0, query_latent_width),
        out_specs=(
            remote_space,
            vmem,
            remote_space,
            remote_space,
            remote_space,
            pl.BlockSpec((tokens, heads * D_V), lambda step: (0, step)),
        ),
        scratch_shapes=[
            pltpu.VMEM(packed, jnp.bfloat16),
            pltpu.VMEM((part, D_NOPE), jnp.bfloat16),
            *(pltpu.VMEM(shape, jnp.bfloat16) for shape in gathered),
            *prefill_scratch(tokens),
            *exchange_sems(peers),
            pltpu.SemaphoreType.DMA((3, 3)),
            pltpu.SemaphoreType.DMA((3, 3)),
            pltpu.SemaphoreType.DMA((3,)),
        ],
        compiler_params=pltpu.CompilerParams(
            vmem_limit_bytes=VMEM_BYTES, collective_id=0, has_side_effects=True
        ),
    )(
        owner[None, :],
        slot[None, :],
        queries,
        latents,
        query_latents,
        rotary,
        positions[None, :],
        frequency,
        *weights,
    )


def last_call(back, answers, gathered, frequency, weights, split):
    peers = answers.shape[0]
    heads, steps, start = split
    groups, part, query_latent_width = gathered[0].shape
    tokens = groups * part
    vmem = pl.BlockSpec(memory_space=pltpu.VMEM)
    return pl.pallas_call(
        functools.partial(last_kernel, heads),
        out_shape=(
            jax.ShapeDtypeStruct((back.shape[1], answers.shape[2]), jnp.bfloat16),
            jax.ShapeDtypeStruct((tokens, steps * heads * D_V), jnp.bfloat16),
        ),
        grid=(steps,),
        in_specs=[vmem, pl.BlockSpec(memory_space=pl.ANY)]
        + [vmem] * 4
        + weight_specs(heads, start, query_latent_width),
        out_specs=(vmem, pl.BlockSpec((tokens, heads * D_V), lambda step: (0, step))),
        scratch_shapes=[
            pltpu.VMEM(answers.shape, jnp.bfloat16),
            *prefill_scratch(tokens),
            *exchange_sems(peers),
        ],
        compiler_params=pltpu.CompilerParams(
            vmem_limit_bytes=VMEM_BYTES, collective_id=1, has_side_effects=True
        ),
    )(back, answers, *gathered, frequency, *weights)


def join_kernel(first_ref, second_ref, decoded_ref, out_ref, decoded_out_ref):
    @pl.when(pl.program_id(0) == 0)
    def _():
        out_ref[...] = first_ref[...]
        decoded_out_ref[...] = decoded_ref[...]

    @pl.when(pl.program_id(0) > 0)
    def _():
        out_ref[...] = second_ref[...]


def join(first, second, decoded):
    tokens, width = first.shape
    total = width + second.shape[1]
    whole = lambda step: (0, 0)
    return pl.pallas_call(
        join_kernel,
        out_shape=(
            jax.ShapeDtypeStruct((tokens, total), jnp.bfloat16),
            jax.ShapeDtypeStruct(decoded.shape, jnp.bfloat16),
        ),
        grid=(total // width,),
        in_specs=[
            pl.BlockSpec((tokens, width), whole),
            pl.BlockSpec((tokens, width), lambda step: (0, jnp.maximum(step - 1, 0))),
            pl.BlockSpec(decoded.shape, whole),
        ],
        out_specs=(
            pl.BlockSpec((tokens, width), lambda step: (0, step)),
            pl.BlockSpec(decoded.shape, whole),
        ),
        compiler_params=pltpu.CompilerParams(vmem_limit_bytes=VMEM_BYTES),
    )(first, second, decoded)


def on_device(
    prompt_query_latents,
    prompt_latents,
    prompt_rotary_keys,
    positions,
    query_up_weight,
    key_up_weight,
    value_up_weight,
    decode_queries,
    decode_owner_index,
    decode_cache_slot,
    latent_cache_rows,
    rotated_cache_keys,
    cache_live_lengths,
):
    row_count = decode_queries.shape[0]
    peers = lax.axis_size("req")
    most = max(2, row_count * 2 // peers)
    half_width = D_ROPE // 2
    frequency = ROPE_BASE ** (-jnp.arange(half_width, dtype=jnp.float32) / half_width)
    frequency = jnp.tile(frequency, 4)[None, :]
    weights = (query_up_weight, key_up_weight, value_up_weight)
    head_count = key_up_weight.shape[1] // D_NOPE
    heads = 4
    steps = head_count // heads
    early = max(1, steps // 4)

    payload, back, *gathered, first_half = first_call(
        decode_owner_index,
        decode_cache_slot,
        decode_queries,
        prompt_latents,
        prompt_query_latents,
        prompt_rotary_keys,
        positions,
        frequency,
        weights,
        (heads, early, 0),
        most,
    )
    answers = decode_attention(
        payload,
        key_up_weight,
        value_up_weight,
        latent_cache_rows,
        rotated_cache_keys,
        cache_live_lengths,
    )
    decode_out, second_half = last_call(
        back, answers, gathered, frequency, weights, (heads, steps - early, early)
    )
    return join(first_half, second_half, decode_out)


def solution(mesh):
    placed = (
        P(("req", "head"), None),
        P(("req", "head"), None),
        P(None, ("req", "head")),
        P(("req", "head")),
        P(None, "head"),
        P(None, "head"),
        P(None, "head"),
        P("req", "head"),
        P("req"),
        P("req"),
        P("req", None, None),
        P("req", None, None),
        P("req"),
    )
    return jax.shard_map(
        on_device,
        mesh=mesh,
        in_specs=placed,
        out_specs=(P("req", "head"), P("req", "head")),
        check_vma=False,
    )
```

```python
import functools
import math

import jax
import jax.numpy as jnp
from jax import lax
from jax.experimental import pallas as pl
from jax.experimental.pallas import tpu as pltpu
from jax.sharding import PartitionSpec as P

D_C = 512
D_NOPE = 128
D_ROPE = 64
D_V = 128
D_Q = D_NOPE + D_ROPE
ROPE_BASE = 10000.0
SCALE = D_Q ** (-0.5)
EXP2_SCALE = SCALE * math.log2(math.e)
MASKED = -1e30
DIGIT = 256
NT = (((1,), (1,)), ((), ()))
TN = (((0,), (0,)), ((), ()))
VMEM_BYTES = 56 * 1024 * 1024


def mm(a, b, dims=(((1,), (0,)), ((), ()))):
    return lax.dot_general(a, b, dims, preferred_element_type=jnp.float32)


def softmax_weights(scores):
    shifted = scores - jnp.max(scores, axis=-1, keepdims=True)
    grown = jnp.exp2(shifted * EXP2_SCALE)
    total = jnp.sum(grown, axis=-1, keepdims=True)
    return (grown * (1.0 / total)).astype(jnp.bfloat16)


def greet(partners):
    barrier = pltpu.get_barrier_semaphore()
    for partner in partners:
        pl.semaphore_signal(
            barrier, inc=1, device_id=partner, device_id_type=pl.DeviceIdType.MESH
        )
    pl.semaphore_wait(barrier, len(partners))


def remote(source, target, send_sem, recv_sem, partner):
    return pltpu.make_async_remote_copy(
        src_ref=source,
        dst_ref=target,
        send_sem=send_sem,
        recv_sem=recv_sem,
        device_id=partner,
        device_id_type=pl.DeviceIdType.MESH,
    )


def peer_at(hop, peers):
    return lax.rem(lax.axis_index("req") + hop, peers)


def exchange_copies(peers, source_ref, target_ref, local_sem, send_sem, recv_sem):
    me = lax.axis_index("req")
    copies = [pltpu.make_async_copy(source_ref.at[me], target_ref.at[me], local_sem)]
    for hop in range(1, peers):
        target = peer_at(hop, peers)
        copies.append(
            remote(
                source_ref.at[target],
                target_ref.at[me],
                send_sem.at[hop],
                recv_sem.at[hop],
                {"req": target},
            )
        )
    return copies


def pack_queries(owner_ref, slot_ref, queries_ref, back_ref, packed_ref):
    peers, most, _ = packed_ref.shape
    rows, width = queries_ref.shape
    owner = owner_ref[...].astype(jnp.float32)
    slot = slot_ref[...].astype(jnp.float32)
    across = jnp.broadcast_to(owner, (rows, rows))
    down = across.T
    before = lax.broadcasted_iota(jnp.int32, (rows, rows), 0) < lax.broadcasted_iota(
        jnp.int32, (rows, rows), 1
    )
    rank = jnp.sum(jnp.where((across == down) & before, 1.0, 0.0), axis=0, keepdims=True)
    place = owner * most + rank
    back_ref[...] = place.astype(jnp.int32)
    index = lax.broadcasted_iota(jnp.int32, (peers * most, rows), 0).astype(jnp.float32)
    placing = index == place
    packed = mm(jnp.where(placing, 1.0, 0.0).astype(jnp.bfloat16), queries_ref[...])
    code = jnp.sum(jnp.where(placing, slot + 1.0, 0.0), axis=1, keepdims=True)
    packed_ref[:, :, :width] = packed.reshape(peers, most, width).astype(jnp.bfloat16)
    packed_ref[:, :, width:] = (
        jnp.broadcast_to(code, (peers * most, 128)).reshape(peers, most, 128).astype(jnp.bfloat16)
    )


def pack_extras(rotary_ref, positions_ref, extras_ref):
    tokens = extras_ref.shape[0]
    rotary = rotary_ref[...].astype(jnp.float32)
    place = jnp.broadcast_to(positions_ref[...].astype(jnp.float32), (D_ROPE, tokens))
    high = jnp.floor(place * (1.0 / DIGIT))
    row = lax.broadcasted_iota(jnp.int32, (D_ROPE, tokens), 0)
    digits = jnp.where(row == 0, high, jnp.where(row == 1, place - high * DIGIT, 0.0))
    extras_ref[...] = jnp.concatenate([rotary, digits], axis=0).T.astype(jnp.bfloat16)


def first_kernel(
    heads,
    owner_ref,
    slot_ref,
    queries_ref,
    latents_in_ref,
    query_latents_in_ref,
    rotary_ref,
    positions_ref,
    frequency_ref,
    query_up_ref,
    key_up_ref,
    value_up_ref,
    payload_ref,
    back_ref,
    query_latents_out_ref,
    latents_out_ref,
    extras_out_ref,
    out_ref,
    packed_ref,
    extras_in_ref,
    query_latents_ref,
    latents_ref,
    extras_ref,
    bias_ref,
    cosine_ref,
    sine_ref,
    key_rope_ref,
    local_sem,
    send_sem,
    recv_sem,
    near_send_sem,
    near_recv_sem,
    keep_sem,
):
    peers = payload_ref.shape[0]
    groups = query_latents_ref.shape[0]
    step = pl.program_id(0)
    group = lax.axis_index("head")
    sibling = group + 1 - 2 * lax.rem(group, 2)
    far = lax.rem(group + groups // 2, groups)
    gathered = (query_latents_ref, latents_ref, extras_ref)
    kept = (query_latents_out_ref, latents_out_ref, extras_out_ref)

    def keeping():
        return [
            pltpu.make_async_copy(source, target, keep_sem.at[index])
            for index, (source, target) in enumerate(zip(gathered, kept))
        ]

    def exchanging():
        return exchange_copies(peers, packed_ref, payload_ref, local_sem, send_sem, recv_sem)

    @pl.when(step == 0)
    def _():
        pack_extras(rotary_ref, positions_ref, extras_in_ref)
        pack_queries(owner_ref, slot_ref, queries_ref, back_ref, packed_ref)
        greet(
            [{"req": peer_at(hop, peers)} for hop in range(1, peers)]
            + [{"head": sibling}, {"head": far}]
        )
        mine = (query_latents_in_ref, latents_in_ref, extras_in_ref)
        near, across = [], []
        for index, (source, target) in enumerate(zip(mine, gathered)):
            for kind, (copies, partner) in enumerate(((across, far), (near, sibling))):
                copies.append(
                    remote(
                        source,
                        target.at[group],
                        near_send_sem.at[index, kind],
                        near_recv_sem.at[index, kind],
                        {"head": partner},
                    )
                )
        for copy in across[::-1]:
            copy.start()
        for copy in near[::-1]:
            copy.start()
        for copy in exchanging():
            copy.start()
        for source, target in zip(mine, gathered):
            target[group] = source[...]

        def pass_on(index):
            target = gathered[index]
            across[index].wait_recv()
            onward = remote(
                target.at[far],
                target.at[far],
                near_send_sem.at[index, 2],
                near_recv_sem.at[index, 2],
                {"head": sibling},
            )
            onward.start()
            return onward

        forward = pass_on(2)
        near[2].wait()
        forward.wait()
        prefill_setup(
            extras_ref, frequency_ref, bias_ref, cosine_ref, sine_ref, key_rope_ref
        )
        forward = [pass_on(1), pass_on(0)]
        for copy in across:
            copy.wait_send()
        for copy in near[:2] + forward:
            copy.wait()
        for copy in keeping():
            copy.start()

    prefill_heads(
        heads,
        query_latents_ref,
        latents_ref,
        query_up_ref,
        key_up_ref,
        value_up_ref,
        out_ref,
        bias_ref,
        cosine_ref,
        sine_ref,
        key_rope_ref,
    )

    @pl.when(step == pl.num_programs(0) - 1)
    def _():
        for copy in keeping() + exchanging():
            copy.wait()


def last_kernel(
    heads,
    back_ref,
    answers_ref,
    query_latents_ref,
    latents_ref,
    extras_ref,
    frequency_ref,
    query_up_ref,
    key_up_ref,
    value_up_ref,
    decoded_ref,
    out_ref,
    landed_ref,
    bias_ref,
    cosine_ref,
    sine_ref,
    key_rope_ref,
    local_sem,
    send_sem,
    recv_sem,
):
    peers, most, width = landed_ref.shape
    step = pl.program_id(0)

    def exchanging():
        return exchange_copies(peers, answers_ref, landed_ref, local_sem, send_sem, recv_sem)

    @pl.when(step == 0)
    def _():
        greet([{"req": peer_at(hop, peers)} for hop in range(1, peers)])
        for copy in exchanging():
            copy.start()
        prefill_setup(
            extras_ref, frequency_ref, bias_ref, cosine_ref, sine_ref, key_rope_ref
        )

    prefill_heads(
        heads,
        query_latents_ref,
        latents_ref,
        query_up_ref,
        key_up_ref,
        value_up_ref,
        out_ref,
        bias_ref,
        cosine_ref,
        sine_ref,
        key_rope_ref,
    )

    @pl.when(step == pl.num_programs(0) - 1)
    def _():
        for copy in exchanging():
            copy.wait()
        blocks = landed_ref[...].astype(jnp.float32).reshape(peers * most, width)
        index = lax.broadcasted_iota(jnp.int32, (peers * most, back_ref.shape[1]), 0)
        wanted = jnp.where(index == back_ref[...], 1.0, 0.0).astype(jnp.bfloat16)
        decoded_ref[...] = mm(wanted, blocks.astype(jnp.bfloat16), TN).astype(jnp.bfloat16)


def exchange_sems(peers):
    return [
        pltpu.SemaphoreType.DMA,
        pltpu.SemaphoreType.DMA((peers,)),
        pltpu.SemaphoreType.DMA((peers,)),
    ]


def decode_kernel(
    slots_per_step,
    head_count,
    lengths_ref,
    payload_ref,
    key_up_ref,
    value_up_ref,
    cache_ref,
    rope_ref,
    out_ref,
    query_ref,
    rope_query_ref,
    latent_out_ref,
    value_ref,
):
    step = pl.program_id(0)
    value_width = value_up_ref.shape[1]
    value_ref[:, pl.ds(pl.multiple_of(step * value_width, value_width), value_width)] = (
        value_up_ref[...]
    )
    width = head_count * D_Q
    slot_count = query_ref.shape[1] // head_count
    chunks = query_ref.shape[0]
    rows = slots_per_step * head_count
    peers, most, _ = payload_ref.shape
    items = peers * most

    def chosen():
        code = payload_ref[:, :, width:].astype(jnp.float32).reshape(items, 128)[:, :1]
        slots = lax.broadcasted_iota(jnp.int32, (items, slot_count), 1).astype(jnp.float32)
        return jnp.where(code == slots + 1.0, 1.0, 0.0).astype(jnp.bfloat16)

    @pl.when(step == 0)
    def _():
        received = payload_ref[:, :, :width].reshape(items, width)
        queries = mm(chosen(), received, TN)
        for head in range(head_count):
            nope = queries[:, head * D_Q : head * D_Q + D_NOPE].astype(jnp.bfloat16)
            latent = mm(nope, key_up_ref[:, head * D_NOPE : (head + 1) * D_NOPE], NT)
            place = pl.ds(head, slot_count, stride=head_count)
            latent = latent.astype(jnp.bfloat16).astype(jnp.float32)
            for chunk in range(chunks):
                query_ref[chunk, place, :] = latent[:, chunk * 128 : (chunk + 1) * 128]
            rope = queries[:, head * D_Q + D_NOPE : (head + 1) * D_Q]
            rope_query_ref[place, :] = jnp.concatenate([rope, rope], axis=1)

    first = step * slots_per_step
    unit = 128 // head_count
    cache_rows = cache_ref.shape[1]
    lanes = lax.broadcasted_iota(jnp.int32, (head_count, cache_rows), 1)
    owner = lax.broadcasted_iota(jnp.int32, (cache_rows, 128), 1) // head_count
    batches = range(0, slots_per_step, unit)
    products = []
    for batch in batches:
        here = pl.ds(pl.multiple_of(step * rows, 128) + batch * head_count, 128)
        columns = jnp.concatenate(
            [query_ref[chunk, here, :].T for chunk in range(chunks)], axis=0
        ).astype(jnp.bfloat16)
        latents = cache_ref[batch : batch + unit].reshape(unit * cache_rows, D_C)
        products.append(mm(latents, columns))
    for batch, product in zip(batches, products):
        here = pl.ds(pl.multiple_of(step * rows, 128) + batch * head_count, 128)
        turned = product[:cache_rows]
        for item in range(1, unit):
            place = slice(item * cache_rows, (item + 1) * cache_rows)
            turned = jnp.where(owner == item, product[place], turned)
        scores = turned.T
        rope_query = rope_query_ref[here, :D_ROPE].astype(jnp.bfloat16)
        parts = []
        for item in range(unit):
            place = slice(item * head_count, (item + 1) * head_count)
            part = scores[place] + mm(rope_query[place], rope_ref[batch + item])
            parts.append(jnp.where(lanes < lengths_ref[first + batch + item], part, MASKED))
        weights = softmax_weights(jnp.concatenate(parts, axis=0))
        latent = jnp.concatenate(
            [
                mm(weights[item * head_count : (item + 1) * head_count], cache_ref[batch + item])
                for item in range(unit)
            ],
            axis=0,
        )
        latent = latent.astype(jnp.bfloat16).astype(jnp.float32)
        for chunk in range(chunks):
            latent_out_ref[chunk, here, :] = latent[:, chunk * 128 : (chunk + 1) * 128]

    @pl.when(step == pl.num_programs(0) - 1)
    def _():
        sending = chosen()
        for head in range(head_count):
            strided = pl.ds(head, slot_count, stride=head_count)
            latent = jnp.concatenate(
                [latent_out_ref[chunk, strided, :] for chunk in range(chunks)], axis=1
            )
            place = slice(head * D_V, (head + 1) * D_V)
            answer = mm(latent.astype(jnp.bfloat16), value_ref[:, place])
            answer = mm(sending, answer.astype(jnp.bfloat16)).astype(jnp.bfloat16)
            out_ref[:, :, place] = answer.reshape(peers, most, D_V)


def decode_attention(payload, key_up, value_up, cache, rope_cache, lengths):
    slot_count, cache_rows, _ = cache.shape
    head_count = key_up.shape[1] // D_NOPE
    per_step = 16
    steps = slot_count // per_step
    peers, most, _ = payload.shape
    whole = lambda step, *_: (0, 0)
    single = lambda step, *_: (0, 0, 0)
    flops = 2 * slot_count * head_count * (2 * D_NOPE * D_C + 17 * cache_rows * D_C)
    block = jax.ShapeDtypeStruct((peers, most, head_count * D_V), jnp.bfloat16)
    return pl.pallas_call(
        functools.partial(decode_kernel, per_step, head_count),
        out_shape=block,
        grid_spec=pltpu.PrefetchScalarGridSpec(
            num_scalar_prefetch=1,
            grid=(steps,),
            in_specs=[
                pl.BlockSpec(payload.shape, single),
                pl.BlockSpec(key_up.shape, whole),
                pl.BlockSpec((D_C, value_up.shape[1] // steps), lambda step, *_: (0, step)),
                pl.BlockSpec((per_step, cache_rows, D_C), lambda step, *_: (step, 0, 0)),
                pl.BlockSpec((per_step, D_ROPE, cache_rows), lambda step, *_: (step, 0, 0)),
            ],
            out_specs=pl.BlockSpec(block.shape, single),
            scratch_shapes=[
                pltpu.VMEM((D_C // 128, slot_count * head_count, 128), jnp.float32),
                pltpu.VMEM((slot_count * head_count, 2 * D_ROPE), jnp.float32),
                pltpu.VMEM((D_C // 128, slot_count * head_count, 128), jnp.float32),
                pltpu.VMEM(value_up.shape, jnp.bfloat16),
            ],
        ),
        compiler_params=pltpu.CompilerParams(vmem_limit_bytes=VMEM_BYTES),
        cost_estimate=pl.CostEstimate(
            flops=flops, bytes_accessed=cache.size * 2 + payload.size * 2, transcendentals=0
        ),
    )(lengths, payload, key_up, value_up, cache, rope_cache)


def lane_marks(tokens):
    lanes = lax.broadcasted_iota(jnp.int32, (tokens, D_NOPE), 1)
    return lanes < D_ROPE, lanes % D_ROPE < D_ROPE // 2


def rotated(values, leading, cosine_ref, sine_ref):
    swapped = jnp.where(
        leading,
        pltpu.roll(values, D_NOPE - D_ROPE // 2, 1),
        pltpu.roll(values, D_ROPE // 2, 1),
    )
    return values * cosine_ref[...] + swapped * sine_ref[...]


def prefill_setup(extras_ref, frequency_ref, bias_ref, cosine_ref, sine_ref, key_rope_ref):
    tokens = bias_ref.shape[0]
    low, leading = lane_marks(tokens)
    extras = extras_ref[...].astype(jnp.float32).reshape(tokens, D_NOPE)
    position = extras[:, D_ROPE : D_ROPE + 1] * DIGIT + extras[:, D_ROPE + 1 : D_ROPE + 2]
    row = lax.broadcasted_iota(jnp.int32, (tokens, tokens), 0).astype(jnp.float32)
    column = lax.broadcasted_iota(jnp.int32, (tokens, tokens), 1).astype(jnp.float32)
    visible = (column <= row) & (column >= row - position)
    bias_ref[...] = jnp.where(visible, 0.0, MASKED)
    angles = position * frequency_ref[...]
    cosine_ref[...] = jnp.cos(angles)
    sines = jnp.sin(angles)
    sine_ref[...] = jnp.where(leading, -sines, sines)
    twice = jnp.where(low, extras, pltpu.roll(extras, D_ROPE, 1))
    turned = rotated(twice, leading, cosine_ref, sine_ref)
    key_rope_ref[...] = turned.T[:D_ROPE].astype(jnp.bfloat16)


def prefill_heads(
    heads,
    query_latents_ref,
    latents_ref,
    query_up_ref,
    key_up_ref,
    value_up_ref,
    out_ref,
    bias_ref,
    cosine_ref,
    sine_ref,
    key_rope_ref,
):
    tokens = bias_ref.shape[0]
    low, leading = lane_marks(tokens)
    query_latents = query_latents_ref[...].reshape(tokens, query_up_ref.shape[0])
    latents = latents_ref[...].reshape(tokens, key_up_ref.shape[0])
    projected = mm(query_latents, query_up_ref[...])
    keys = mm(latents, key_up_ref[...]).astype(jnp.bfloat16).T
    values = mm(latents, value_up_ref[...]).astype(jnp.bfloat16)
    key_rope = key_rope_ref[...]
    none = jnp.zeros((D_ROPE, tokens), jnp.bfloat16)
    tile = min(256, tokens)
    work = []
    for pair in range(heads // 2):
        base = pair * 2 * D_Q
        left = projected[:, base : base + D_NOPE].astype(jnp.bfloat16)
        middle = projected[:, base + D_NOPE : base + 2 * D_NOPE]
        middle = jnp.where(low, rotated(middle, leading, cosine_ref, sine_ref), middle).astype(jnp.bfloat16)
        right = projected[:, base + 2 * D_NOPE : base + 3 * D_NOPE]
        right = jnp.where(low, right, rotated(right, leading, cosine_ref, sine_ref)).astype(jnp.bfloat16)
        even = keys[2 * pair * D_NOPE : (2 * pair + 1) * D_NOPE]
        odd = keys[(2 * pair + 1) * D_NOPE : (2 * pair + 2) * D_NOPE]
        both = (
            (
                jnp.concatenate([left, middle], axis=1),
                jnp.concatenate([even, key_rope, none], axis=0),
            ),
            (
                jnp.concatenate([middle, right], axis=1),
                jnp.concatenate([none, odd, key_rope], axis=0),
            ),
        )
        for side, (query, key) in enumerate(both):
            place = slice((2 * pair + side) * D_V, (2 * pair + side + 1) * D_V)
            for begin in range(0, tokens, tile):
                work.append((query, key, place, begin, begin + tile))

    def score(query, key, place, begin, end):
        return mm(query[begin:end], key[:, :end]) + bias_ref[begin:end, :end]

    scores = score(*work[0])
    for index, (_, _, place, begin, end) in enumerate(work):
        following = score(*work[index + 1]) if index + 1 < len(work) else None
        weights = softmax_weights(scores)
        out_ref[begin:end, place] = mm(weights, values[:end, place]).astype(jnp.bfloat16)
        scores = following


def prefill_scratch(tokens):
    return [
        pltpu.VMEM((tokens, tokens), jnp.float32),
        pltpu.VMEM((tokens, D_NOPE), jnp.float32),
        pltpu.VMEM((tokens, D_NOPE), jnp.float32),
        pltpu.VMEM((D_ROPE, tokens), jnp.bfloat16),
    ]


def weight_specs(heads, start, query_latent_width):
    across = lambda step: (0, step + start)
    return [
        pl.BlockSpec((query_latent_width, heads * D_Q), across),
        pl.BlockSpec((D_C, heads * D_NOPE), across),
        pl.BlockSpec((D_C, heads * D_V), across),
    ]


def first_call(
    owner, slot, queries, latents, query_latents, rotary, positions, frequency, weights, split, most
):
    peers, groups = lax.axis_size("req"), lax.axis_size("head")
    heads, steps, _ = split
    rows, width = queries.shape
    part, query_latent_width = query_latents.shape
    tokens = part * groups
    vmem = pl.BlockSpec(memory_space=pltpu.VMEM)
    remote_space = pl.BlockSpec(memory_space=pl.ANY)
    packed = (peers, most, width + 128)
    gathered = [
        (groups, part, query_latent_width),
        (groups, part, D_C),
        (groups, part, D_NOPE),
    ]
    return pl.pallas_call(
        functools.partial(first_kernel, heads),
        out_shape=(
            jax.ShapeDtypeStruct(packed, jnp.bfloat16),
            jax.ShapeDtypeStruct((1, rows), jnp.int32),
            *(jax.ShapeDtypeStruct(shape, jnp.bfloat16) for shape in gathered),
            jax.ShapeDtypeStruct((tokens, steps * heads * D_V), jnp.bfloat16),
        ),
        grid=(steps,),
        in_specs=[vmem] * 8 + weight_specs(heads, 0, query_latent_width),
        out_specs=(
            remote_space,
            vmem,
            remote_space,
            remote_space,
            remote_space,
            pl.BlockSpec((tokens, heads * D_V), lambda step: (0, step)),
        ),
        scratch_shapes=[
            pltpu.VMEM(packed, jnp.bfloat16),
            pltpu.VMEM((part, D_NOPE), jnp.bfloat16),
            *(pltpu.VMEM(shape, jnp.bfloat16) for shape in gathered),
            *prefill_scratch(tokens),
            *exchange_sems(peers),
            pltpu.SemaphoreType.DMA((3, 3)),
            pltpu.SemaphoreType.DMA((3, 3)),
            pltpu.SemaphoreType.DMA((3,)),
        ],
        compiler_params=pltpu.CompilerParams(
            vmem_limit_bytes=VMEM_BYTES, collective_id=0, has_side_effects=True
        ),
    )(
        owner[None, :],
        slot[None, :],
        queries,
        latents,
        query_latents,
        rotary,
        positions[None, :],
        frequency,
        *weights,
    )


def last_call(back, answers, gathered, frequency, weights, split):
    peers = answers.shape[0]
    heads, steps, start = split
    groups, part, query_latent_width = gathered[0].shape
    tokens = groups * part
    vmem = pl.BlockSpec(memory_space=pltpu.VMEM)
    return pl.pallas_call(
        functools.partial(last_kernel, heads),
        out_shape=(
            jax.ShapeDtypeStruct((back.shape[1], answers.shape[2]), jnp.bfloat16),
            jax.ShapeDtypeStruct((tokens, steps * heads * D_V), jnp.bfloat16),
        ),
        grid=(steps,),
        in_specs=[vmem, pl.BlockSpec(memory_space=pl.ANY)]
        + [vmem] * 4
        + weight_specs(heads, start, query_latent_width),
        out_specs=(vmem, pl.BlockSpec((tokens, heads * D_V), lambda step: (0, step))),
        scratch_shapes=[
            pltpu.VMEM(answers.shape, jnp.bfloat16),
            *prefill_scratch(tokens),
            *exchange_sems(peers),
        ],
        compiler_params=pltpu.CompilerParams(
            vmem_limit_bytes=VMEM_BYTES, collective_id=1, has_side_effects=True
        ),
    )(back, answers, *gathered, frequency, *weights)


def join_kernel(first_ref, second_ref, decoded_ref, out_ref, decoded_out_ref):
    @pl.when(pl.program_id(0) == 0)
    def _():
        out_ref[...] = first_ref[...]
        decoded_out_ref[...] = decoded_ref[...]

    @pl.when(pl.program_id(0) > 0)
    def _():
        out_ref[...] = second_ref[...]


def join(first, second, decoded):
    tokens, width = first.shape
    total = width + second.shape[1]
    whole = lambda step: (0, 0)
    return pl.pallas_call(
        join_kernel,
        out_shape=(
            jax.ShapeDtypeStruct((tokens, total), jnp.bfloat16),
            jax.ShapeDtypeStruct(decoded.shape, jnp.bfloat16),
        ),
        grid=(total // width,),
        in_specs=[
            pl.BlockSpec((tokens, width), whole),
            pl.BlockSpec((tokens, width), lambda step: (0, jnp.maximum(step - 1, 0))),
            pl.BlockSpec(decoded.shape, whole),
        ],
        out_specs=(
            pl.BlockSpec((tokens, width), lambda step: (0, step)),
            pl.BlockSpec(decoded.shape, whole),
        ),
        compiler_params=pltpu.CompilerParams(vmem_limit_bytes=VMEM_BYTES),
    )(first, second, decoded)


def on_device(
    prompt_query_latents,
    prompt_latents,
    prompt_rotary_keys,
    positions,
    query_up_weight,
    key_up_weight,
    value_up_weight,
    decode_queries,
    decode_owner_index,
    decode_cache_slot,
    latent_cache_rows,
    rotated_cache_keys,
    cache_live_lengths,
):
    row_count = decode_queries.shape[0]
    peers = lax.axis_size("req")
    most = max(2, row_count * 2 // peers)
    half_width = D_ROPE // 2
    frequency = ROPE_BASE ** (-jnp.arange(half_width, dtype=jnp.float32) / half_width)
    frequency = jnp.tile(frequency, 4)[None, :]
    weights = (query_up_weight, key_up_weight, value_up_weight)
    head_count = key_up_weight.shape[1] // D_NOPE
    heads = 4
    steps = head_count // heads
    early = max(1, steps // 4)

    payload, back, *gathered, first_half = first_call(
        decode_owner_index,
        decode_cache_slot,
        decode_queries,
        prompt_latents,
        prompt_query_latents,
        prompt_rotary_keys,
        positions,
        frequency,
        weights,
        (heads, early, 0),
        most,
    )
    answers = decode_attention(
        payload,
        key_up_weight,
        value_up_weight,
        latent_cache_rows,
        rotated_cache_keys,
        cache_live_lengths,
    )
    decode_out, second_half = last_call(
        back, answers, gathered, frequency, weights, (heads, steps - early, early)
    )
    return join(first_half, second_half, decode_out)


def solution(mesh):
    placed = (
        P(("req", "head"), None),
        P(("req", "head"), None),
        P(None, ("req", "head")),
        P(("req", "head")),
        P(None, "head"),
        P(None, "head"),
        P(None, "head"),
        P("req", "head"),
        P("req"),
        P("req"),
        P("req", None, None),
        P("req", None, None),
        P("req"),
    )
    return jax.shard_map(
        on_device,
        mesh=mesh,
        in_specs=placed,
        out_specs=(P("req", "head"), P("req", "head")),
        check_vma=False,
    )
```
